128 devices in a mesh: pw: 32 (over x, z, y_hi), band: 4 (over y_lo, core).
Axes of the slice: x: 4, y: 4 (y_hi: 2, y_lo: 2; y = y_hi * 2 + y_lo), z: 4, core: 2. Of those that a mesh axis runs over, the one named last changes fastest.
Arguments:
- basis_set: bfloat16 [24576, 2048], P('pw'), may hold values from -0.078125 to 0.078125
- densities: bfloat16 [24576, 4096], P('pw', 'band'), may hold values from -135 to 135
- pair_gaps: float32 [4096], P('band'), may hold values from 0.002 to 500
- frequencies: float32 [16], replicated, may hold values from 0.01 to 100
Outputs:
- polarizability: float32 [16, 2048, 2048], P(None, 'pw', 'band')
- projected: bfloat16 [2048, 4096], P('pw', 'band')
The draws below stay inside these ranges and needn't reach their ends.
All inputs are finite; a program needn't handle non-finite values.
Results may differ from the reference program's by a relative error of at most 0.011.
Values may be sent and summed in bfloat16 or wider, within the bound.
A program may use at most 128 MiB of HBM per device.

```python
import jax
import jax.numpy as jnp
from jax import lax

NPW = 24576
NB = 2048
NFREQ = 16
PAIRS = 4096


def shared_gaps(key):
    unit_draw = jax.random.uniform(jax.random.fold_in(key, 7), (PAIRS,), jnp.float32)
    return 0.002 * jnp.exp(unit_draw * jnp.log(250000.0))


def draw_pair_gaps(key, part):
    return shared_gaps(key).astype(jnp.float32)


def draw_densities(key, part):
    energy_gaps = shared_gaps(key)
    inner_key = jax.random.fold_in(key, 13)
    values = jax.random.truncated_normal(inner_key, -6.0, 6.0, (NPW, PAIRS), jnp.float32)
    return (values * jnp.sqrt(energy_gaps)[None, :]).astype(jnp.bfloat16)


def draw_frequencies(key, part):
    jitter = jax.random.uniform(jax.random.fold_in(key, 19), (NFREQ,), jnp.float32)
    position = (jnp.arange(NFREQ, dtype=jnp.float32) + jitter) / NFREQ
    return (0.01 * jnp.exp(position * jnp.log(10000.0))).astype(jnp.float32)


def raised(values, rng, source, target, shards_of, factor):
    def block_of(axis_at):
        return (jnp.arange(values.shape[axis_at]) // (values.shape[axis_at] // shards_of)).reshape((-1,) + (1,) * (values.ndim - 1 - axis_at))

    first = jax.random.permutation(rng, shards_of)[block_of(target)]
    far = (block_of(target) + shards_of // 2) % shards_of
    return jnp.where((block_of(source) == first) | (block_of(source) == far), factor * values, values)


def level_of(key, dims, pieces, low, largest):
    def one(dim, blocks):
        heights = jax.random.uniform(jax.random.fold_in(jax.random.fold_in(key, 6), dim), (blocks,), jnp.float32, low / len(pieces), largest / len(pieces))
        return jnp.repeat(jnp.exp(heights), dims[dim] // blocks).reshape((-1,) + (1,) * (len(dims) - dim - 1))

    factor_of = one(*pieces[0])
    for cut in pieces[1:]:
        factor_of = factor_of * one(*cut)
    return factor_of


def bell_draw_with(key, dims, spread, bound, shards, heavy, kind=jnp.bfloat16):
    array = spread * jax.random.normal(key, dims, jnp.float32)
    if shards:
        array = array * level_of(key, dims, shards, -0.22, 0.18)
    return jnp.clip(raised(array, jax.random.fold_in(key, 3), *heavy), -bound, bound).astype(kind)


def setup_inputs(seed: int = 0) -> dict:
    keys = jax.random.split(jax.random.key(seed), 5)
    return {
        "basis_set": bell_draw_with(keys[0], (NPW, NB), NPW ** -0.5, 0.078125, ((0, 32),), (0, 1, 32, 2.75)),
        "densities": draw_densities(jax.random.fold_in(keys[4], 71), 0),
        "pair_gaps": draw_pair_gaps(jax.random.fold_in(keys[4], 71), 0),
        "frequencies": draw_frequencies(jax.random.fold_in(keys[4], 71), 0),
    }


def reference(basis_set, densities, pair_gaps, frequencies):
    projected = lax.dot_general(basis_set, densities, (((0,), (0,)), ((), ())), preferred_element_type=jnp.float32).astype(jnp.bfloat16)
    weights = (-4.0 / PAIRS) * pair_gaps[None, :] / (pair_gaps[None, :] ** 2 + frequencies[:, None] ** 2)

    def single(weight_row):
        scaled = (weight_row[None, :] * projected.astype(jnp.float32)).astype(jnp.bfloat16)
        return jnp.dot(scaled, projected.T, preferred_element_type=jnp.float32)

    polarizability = lax.map(single, weights)
    return polarizability, projected
```

```python
import functools

import jax
import jax.numpy as jnp
from jax import lax
from jax.experimental import pallas as pl
from jax.experimental.pallas import tpu as pltpu
from jax.sharding import PartitionSpec as P

MESH = pl.DeviceIdType.MESH
F32, BF16 = jnp.float32, jnp.bfloat16

NK = 768
NB = 2048
NP = 1024
NFREQ = 16
PAIRS = 4096
NBT = 2
W = NP // NBT
H = W // 2
Q = W // 4
NSEM = 96


def device(x, z, yh, yl, c):
    return ((x * 4 + z) * 2 + yh, yl * 2 + c)


def kernel(
    basis_hbm, dens_hbm, gaps, freq,
    pol, proj,
    basis, dens, bt,
    own_f32, s1_recv, s1_far, s1_near, s1_sum,
    s2_send, s2_recv,
    t_send, t_recv, y_send, y_recv,
    ib, gap_all, wts, scaled, jb,
    load_sem, send_sem, recv_sem, home_sem,
):
    pw, g = lax.axis_index("pw"), lax.axis_index("band")
    x, z, yh = pw // 8, (pw // 2) % 4, pw % 2
    yl, c = g // 2, g % 2
    me8 = yh * 4 + g

    loads = [
        pltpu.make_async_copy(basis_hbm, basis, load_sem.at[0]),
        pltpu.make_async_copy(dens_hbm, dens, load_sem.at[1]),
    ]
    for load in loads:
        load.start()

    def along(axis, d):
        if axis == "x":
            return device((x + d) % 4, z, yh, yl, c)
        return device(x, (z + d) % 4, yh, yl, c)

    def beside(d):
        o = (me8 + d) % 8
        return device(x, z, o // 4, (o % 4) // 2, o % 2)

    barrier = pltpu.get_barrier_semaphore()
    peers = [along(a, d) for a in "xz" for d in (1, 2, 3)] + [beside(d) for d in range(1, 8)]
    for peer in peers:
        pl.semaphore_signal(barrier, inc=1, device_id=peer, device_id_type=MESH)
    pl.semaphore_wait(barrier, len(peers))

    drains = []
    count = [0]

    def slot():
        count[0] += 1
        assert count[0] <= NSEM
        return count[0] - 1

    def copy_to(src, dst, sem, to, recv=None):
        return pltpu.make_async_remote_copy(
            src_ref=src, dst_ref=dst, send_sem=send_sem.at[sem],
            recv_sem=recv_sem.at[sem] if recv is None else recv,
            device_id=to, device_id_type=MESH,
        )

    def send(src, dst, sem, to, recv=None):
        cp = copy_to(src, dst, sem, to, recv)
        cp.start()
        drains.append((None, cp))
        return cp

    def send_if(cond, src, dst, sem, to, recv=None):
        cp = copy_to(src, dst, sem, to, recv)
        pl.when(cond)(cp.start)
        drains.append((cond, cp))
        return cp

    gap_all[g] = gaps[...]
    gap_sems = [slot() for _ in range(3)]
    gap_copies = []
    for d in range(1, 4):
        o = (g + d) % 4
        gap_copies.append(
            send(gaps, gap_all.at[g], gap_sems[d - 1], device(x, z, yh, o // 2, o % 2))
        )

    loads[0].wait()
    for i in range(16):
        bt[i // 4, i % 4] = basis[:, i * 128 : (i + 1) * 128].T
    loads[1].wait()

    def block(axis, q, lo, width):
        rows = bt[q] if axis == "x" else bt[:, q]
        return jnp.dot(
            rows.reshape(512, NK), dens[:, lo : lo + width], preferred_element_type=F32
        )

    here = {"x": x, "z": z}
    sem1 = {}

    def first_start(b, axis):
        h = 0 if axis == "x" else 1
        me, lo = here[axis], b * W + h * H
        sems = [slot() for _ in range(6)]
        sem1[b, axis] = sems
        far, near = s1_far.at[b, h], s1_near.at[b, h]
        value = block(axis, (me + 2) % 4, lo, H).astype(BF16)
        far[0] = value[:, :Q]
        far[1] = value[:, Q:]
        recv = s1_recv.at[b, h]
        copies = [
            send(far.at[0], recv.at[0], sems[0], along(axis, 1)),
            send(far.at[1], recv.at[1], sems[1], along(axis, 3)),
        ]
        value = block(axis, (me + 1) % 4, lo, H)
        near[1] = value[:, Q:].astype(BF16)
        copies.append(send(near.at[1], recv.at[3], sems[3], along(axis, 1)))
        own_f32[b, h, 0] = value[:, :Q]
        value = block(axis, (me + 3) % 4, lo, H)
        near[2] = value[:, :Q].astype(BF16)
        copies.append(send(near.at[2], recv.at[4], sems[4], along(axis, 3)))
        own_f32[b, h, 1] = value[:, Q:]
        sem1[b, axis] = (sems, copies)

    def first_own(b, axis):
        h = 0 if axis == "x" else 1
        me, lo = here[axis], b * W + h * H
        s1_sum[b, h] = block(axis, me, lo, H)

    def first_forward(b, axis):
        h = 0 if axis == "x" else 1
        sems, copies = sem1[b, axis]
        near, recv = s1_near.at[b, h], s1_recv.at[b, h]
        copies[0].wait_recv()
        near[0] = (own_f32[b, h, 0] + recv[0].astype(F32)).astype(BF16)
        copies.append(send(near.at[0], recv.at[2], sems[2], along(axis, 1)))
        copies[1].wait_recv()
        near[3] = (own_f32[b, h, 1] + recv[1].astype(F32)).astype(BF16)
        copies.append(send(near.at[3], recv.at[5], sems[5], along(axis, 3)))

    def first_end(b, axis):
        h = 0 if axis == "x" else 1
        recv = s1_recv.at[b, h]
        for cp in sem1[b, axis][1][2:]:
            cp.wait_recv()
        total = s1_sum.at[b, h]
        total[:, :Q] = total[:, :Q] + recv[2].astype(F32) + recv[4].astype(F32)
        total[:, Q:] = total[:, Q:] + recv[3].astype(F32) + recv[5].astype(F32)

    sem2 = {}

    def second_start(b, axis):
        h = 0 if axis == "x" else 1
        other = "z" if axis == "x" else "x"
        me = here[other]
        sems = [slot() for _ in range(3)]
        copies = []
        for i, d in enumerate((2, 1, 3)):
            start = pl.multiple_of((me + d) % 4 * 128, 128)
            s2_send[b, h, i] = s1_sum[b, h, pl.ds(start, 128), :].astype(BF16)
            copies.append(
                send(s2_send.at[b, h, i], s2_recv.at[b, h, i], sems[i], along(other, d))
            )
        sem2[b, axis] = copies

    def second_end(b, axis):
        h = 0 if axis == "x" else 1
        other = "z" if axis == "x" else "x"
        for cp in sem2[b, axis]:
            cp.wait_recv()
        start = pl.multiple_of(here[other] * 128, 128)
        total = s1_sum[b, h, pl.ds(start, 128), :]
        for i in range(3):
            total = total + s2_recv[b, h, i].astype(F32)
        t_send[b, :, h * H : (h + 1) * H] = total.astype(BF16)
        own = pl.multiple_of(yh * 64, 64)
        s1_sum[b, h, pl.ds(0, 128), :] = total
        y_send[b, :, h * H : (h + 1) * H] = s1_sum[
            b, h, pl.ds(pl.multiple_of((1 - yh) * 64, 64), 64), :
        ].astype(BF16)
        s1_sum[b, h, pl.ds(128, 64), :] = s1_sum[b, h, pl.ds(own, 64), :]

    is_home = g == x
    plane = yl * 2 + c
    step = 1 - 2 * (plane % 2)
    rel = (x - plane + 4) % 4
    is_source = rel == 0
    is_out1 = rel == (4 - step) % 4
    pair_to = device((plane + step + 4) % 4, z, yh, yl, c)
    out1_to = device((plane - step + 4) % 4, z, yh, yl, c)
    out2_to = device((plane + 2) % 4, z, yh, yl, c)

    sem_y = {}

    def third_start(b):
        homes = []
        for t in range(2):
            sem = slot()
            target8 = t * 4 + x
            mine = me8 == target8
            send_if(
                jnp.logical_not(mine), t_send.at[b], t_recv.at[b, me8], sem,
                device(x, z, t, x // 2, x % 2), recv=home_sem.at[b, me8],
            )

            @pl.when(mine)
            def _():
                t_recv[b, me8] = t_send[b]

        sem = slot()
        sem_y[b] = send(y_send.at[b], y_recv.at[b], sem, beside(4))

    sem_i = {}

    def rows_start(b):
        sem_y[b].wait_recv()
        for h in range(2):
            sl = slice(h * H, (h + 1) * H)
            value = s1_sum[b, h, pl.ds(128, 64), :] + y_recv[b, :, sl].astype(F32)
            proj[:, b * W + h * H : b * W + (h + 1) * H] = value.astype(BF16)
            ib[b, g, :, sl] = value.astype(BF16)
        copies = []
        for d in range(1, 4):
            o = (g + d) % 4
            sem = slot()
            copies.append(
                send(ib.at[b, g], ib.at[b, g], sem, device(x, z, yh, o // 2, o % 2))
            )
        sem_i[b] = copies

    def weigh(b):
        if b == 0:
            for cp in gap_copies:
                cp.wait_recv()
        square = freq[...] * freq[...]
        for gg in range(4):
            gap = gap_all[gg, :, b * W : (b + 1) * W]
            wts[b, gg // 2, :, (gg % 2) * W : (gg % 2 + 1) * W] = (
                (-4.0 / PAIRS) * gap / (gap * gap + square)
            )

    def scale(b):
        for cp in sem_i[b]:
            cp.wait_recv()
        for h in range(2):
            for e in range(2):
                sl = slice(e * W, (e + 1) * W)
                rows = ib[b, 2 * h + e].astype(F32)

                def at(k, _, h=h, sl=sl, rows=rows):
                    start = pl.multiple_of(k * 64, 64)
                    scaled[b, h, pl.ds(start, 64), sl] = (
                        wts[b, h, pl.ds(k, 1), sl] * rows
                    ).astype(BF16)
                    return 0

                lax.fori_loop(0, NFREQ, at, 0)

    sem_g = {}
    zn = [z, (z + 3) % 4, (z + 1) % 4, (z + 2) % 4]

    def wait_in(dst, sem, to):
        copy_to(dst, dst, sem, to).wait_recv()

    def gather1(b):
        ss = {name: slot() for name in ("x1", "x1o", "a1", "b1", "c1", "d1", "a2", "b2", "c2", "d2")}
        for i in range(4):
            ss["x2", i] = slot()
            ss["x2o", i] = slot()
        sem_g[b] = ss

        @pl.when(is_home)
        def _():
            for d in range(1, 8):
                o = (me8 + d) % 8
                copy_to(
                    t_recv.at[b, o], t_recv.at[b, o], 0, along("x", 1),
                    recv=home_sem.at[b, o],
                ).wait_recv()
            for gg in range(4):
                total = t_recv[b, gg].astype(F32) + t_recv[b, 4 + gg].astype(F32)
                jb[b, z, gg // 2, :, (gg % 2) * W : (gg % 2 + 1) * W] = total.astype(BF16)

        one, two = jb.at[b, z, 0], jb.at[b, z, 1]
        send_if(is_source, one, one, ss["x1"], out1_to)
        send_if(is_source, two, two, ss["a2"], along("z", 1))
        send_if(is_source, two, two, ss["b2"], along("z", 3))
        send_if(is_source, one, one, ss["x1o"], pair_to, recv=recv_sem.at[ss["x1"]])

    def gather2(b):
        ss = sem_g[b]
        one, two = jb.at[b, z, 0], jb.at[b, z, 1]

        @pl.when(jnp.logical_not(is_source))
        def _():
            wait_in(one, ss["x1"], along("x", 1))

        fwd = copy_to(one, one, ss["x1"], out2_to)
        pl.when(is_out1)(fwd.start)
        drains.append((is_out1, fwd))
        send(one, one, ss["a1"], along("z", 1))
        send(one, one, ss["b1"], along("z", 3))
        spread2(b, 0)

    def spread2(b, i):
        ss = sem_g[b]
        part = jb.at[b, zn[i], 1]
        send_if(is_source, part, part, ss["x2", i], out1_to)
        send_if(is_source, part, part, ss["x2o", i], pair_to, recv=recv_sem.at[ss["x2", i]])

    def pass2(b, i):
        ss = sem_g[b]
        part = jb.at[b, zn[i], 1]

        @pl.when(jnp.logical_not(is_source))
        def _():
            wait_in(part, ss["x2", i], along("x", 1))

        fwd = copy_to(part, part, ss["x2", i], out2_to)
        pl.when(is_out1)(fwd.start)
        drains.append((is_out1, fwd))

    def ring_mid(b, h, cond):
        ss = sem_g[b]
        n = str(h + 1)

        def go():
            wait_in(jb.at[b, zn[1], h], ss["a" + n], along("z", 1))

        def go2():
            wait_in(jb.at[b, zn[2], h], ss["b" + n], along("z", 1))

        lower, upper = jb.at[b, zn[1], h, pl.ds(0, 64)], jb.at[b, zn[2], h, pl.ds(64, 64)]
        if cond is None:
            go()
            send(lower, lower, ss["c" + n], along("z", 1))
            go2()
            send(upper, upper, ss["d" + n], along("z", 3))
        else:
            pl.when(cond)(go)
            send_if(cond, lower, lower, ss["c" + n], along("z", 1))
            pl.when(cond)(go2)
            send_if(cond, upper, upper, ss["d" + n], along("z", 3))

    def ring_end(b, h, cond):
        ss = sem_g[b]
        n = str(h + 1)

        def go():
            wait_in(jb.at[b, zn[3], h, pl.ds(0, 64)], ss["c" + n], along("z", 1))
            wait_in(jb.at[b, zn[3], h, pl.ds(64, 64)], ss["d" + n], along("z", 1))

        if cond is None:
            go()
        else:
            pl.when(cond)(go)

    def gather3(b):
        ring_mid(b, 1, is_source)
        spread2(b, 1)
        spread2(b, 2)
        ring_mid(b, 0, None)
        pass2(b, 0)

    def gather4(b):
        ring_end(b, 1, is_source)
        spread2(b, 3)
        pass2(b, 1)
        pass2(b, 2)

    def gather5(b):
        ring_end(b, 0, None)
        pass2(b, 3)

    def multiply(b, h, i, first=False):
        col = pl.multiple_of(zn[i] * 128, 128)
        value = lax.dot_general(
            scaled[b, h], jb[b, zn[i], h], (((1,), (1,)), ((), ())), preferred_element_type=F32
        )
        if first:
            pol[:, pl.ds(col, 128)] = value
        else:
            pol[:, pl.ds(col, 128)] += value

    batches = range(NBT)
    for b in batches:
        for axis in "xz":
            first_start(b, axis)
    for b in batches:
        for axis in "xz":
            first_forward(b, axis)
    for b in batches:
        for axis in "xz":
            first_own(b, axis)
    for b in batches:
        for axis in "xz":
            first_end(b, axis)
            second_start(b, axis)
        weigh(b)
    for b in batches:
        for axis in "xz":
            second_end(b, axis)
        third_start(b)
    for b in batches:
        gather1(b)
        rows_start(b)
        gather2(b)
    for b in batches:
        gather3(b)
        scale(b)
    for b in batches:
        gather4(b)
        for i in range(3):
            multiply(b, 0, i, first=b == 0)
        for i in range(3):
            multiply(b, 1, i)
    for b in batches:
        gather5(b)
        multiply(b, 0, 3, first=b == 0)
        multiply(b, 1, 3)

    for cond, cp in drains:
        if cond is None:
            cp.wait_send()
        else:
            pl.when(cond)(cp.wait_send)


def on_device(basis_set, densities, pair_gaps, frequencies):
    any_, vmem = pl.BlockSpec(memory_space=pl.ANY), pl.BlockSpec(memory_space=pltpu.VMEM)
    pol, proj = pl.pallas_call(
        kernel,
        out_shape=(
            jax.ShapeDtypeStruct((NFREQ * 64, 512), F32),
            jax.ShapeDtypeStruct((64, NP), BF16),
        ),
        in_specs=[any_, any_, vmem, vmem],
        out_specs=(vmem, vmem),
        scratch_shapes=[
            pltpu.VMEM((NK, NB), BF16),
            pltpu.VMEM((NK, NP), BF16),
            pltpu.VMEM((4, 4, 128, NK), BF16),
            pltpu.VMEM((NBT, 2, 2, 512, Q), F32),
            pltpu.VMEM((NBT, 2, 6, 512, Q), BF16),
            pltpu.VMEM((NBT, 2, 2, 512, Q), BF16),
            pltpu.VMEM((NBT, 2, 4, 512, Q), BF16),
            pltpu.VMEM((NBT, 2, 512, H), F32),
            pltpu.VMEM((NBT, 2, 3, 128, H), BF16),
            pltpu.VMEM((NBT, 2, 3, 128, H), BF16),
            pltpu.VMEM((NBT, 128, W), BF16),
            pltpu.VMEM((NBT, 8, 128, W), BF16),
            pltpu.VMEM((NBT, 64, W), BF16),
            pltpu.VMEM((NBT, 64, W), BF16),
            pltpu.VMEM((NBT, 4, 64, W), BF16),
            pltpu.VMEM((4, 1, NP), F32),
            pltpu.VMEM((NBT, 2, NFREQ, 2 * W), F32),
            pltpu.VMEM((NBT, 2, NFREQ * 64, 2 * W), BF16),
            pltpu.VMEM((NBT, 4, 2, 128, 2 * W), BF16),
            pltpu.SemaphoreType.DMA((2,)),
            pltpu.SemaphoreType.DMA((NSEM,)),
            pltpu.SemaphoreType.DMA((NSEM,)),
            pltpu.SemaphoreType.DMA((NBT, 8)),
        ],
        compiler_params=pltpu.CompilerParams(
            collective_id=0, has_side_effects=True, vmem_limit_bytes=56 * 2**20
        ),
    )(basis_set, densities, pair_gaps.reshape(1, NP), frequencies.reshape(NFREQ, 1))
    return pol.reshape(NFREQ, 64, 512), proj


def solution(mesh):
    in_specs = (P("pw", None), P("pw", "band"), P("band"), P())
    out_specs = (P(None, "pw", "band"), P("pw", "band"))
    return jax.shard_map(
        on_device, mesh=mesh, in_specs=in_specs, out_specs=out_specs, check_vma=False
    )
```

```python
import functools

import jax
import jax.numpy as jnp
from jax import lax
from jax.experimental import pallas as pl
from jax.experimental.pallas import tpu as pltpu
from jax.sharding import PartitionSpec as P

MESH = pl.DeviceIdType.MESH
F32, BF16 = jnp.float32, jnp.bfloat16

NK = 768
NB = 2048
NP = 1024
NFREQ = 16
PAIRS = 4096
NBT = 2
W = NP // NBT
H = W // 2
Q = W // 4
NSEM = 160


def device(x, z, yh, yl, c):
    return ((x * 4 + z) * 2 + yh, yl * 2 + c)


def kernel(
    basis_hbm, dens_hbm, gaps, freq,
    pol, proj,
    basis, dens, bt,
    own_f32, s1_recv, s1_far, s1_near, s1_sum,
    s2_send, s2_recv,
    t_own, y_send, y_recv,
    ib, gap_all, wts, scaled, jb,
    load_sem, send_sem, recv_sem, home_sem, row_sem,
):
    pw, g = lax.axis_index("pw"), lax.axis_index("band")
    x, z, yh = pw // 8, (pw // 2) % 4, pw % 2
    yl, c = g // 2, g % 2
    me8 = yh * 4 + g

    def fetch(src, dst, cols, n):
        return pltpu.make_async_copy(src.at[:, cols], dst.at[:, cols], load_sem.at[n])

    loads = [fetch(dens_hbm, dens, pl.ds(0, W), 0)]
    for n, d in enumerate((2, 0, 1, 3)):
        cols = pl.ds(pl.multiple_of((x + d) % 4 * 512, 512), 512)
        loads.append(fetch(basis_hbm, basis, cols, n + 1))
    loads.append(fetch(dens_hbm, dens, pl.ds(W, NP - W), 5))
    for load in loads:
        load.start()

    def along(axis, d):
        if axis == "x":
            return device((x + d) % 4, z, yh, yl, c)
        return device(x, (z + d) % 4, yh, yl, c)

    def beside(d):
        o = (me8 + d) % 8
        return device(x, z, o // 4, (o % 4) // 2, o % 2)

    barrier = pltpu.get_barrier_semaphore()
    peers = [along(a, d) for a in "xz" for d in (1, 2, 3)] + [beside(d) for d in range(1, 8)]
    for peer in peers:
        pl.semaphore_signal(barrier, inc=1, device_id=peer, device_id_type=MESH)
    pl.semaphore_wait(barrier, len(peers))

    drains = []
    count = [0]

    def slot():
        count[0] += 1
        assert count[0] <= NSEM
        return count[0] - 1

    def copy_to(src, dst, sem, to, recv=None):
        return pltpu.make_async_remote_copy(
            src_ref=src, dst_ref=dst, send_sem=send_sem.at[sem],
            recv_sem=recv_sem.at[sem] if recv is None else recv,
            device_id=to, device_id_type=MESH,
        )

    def send(src, dst, sem, to, recv=None):
        cp = copy_to(src, dst, sem, to, recv)
        cp.start()
        drains.append((None, cp))
        return cp

    def send_if(cond, src, dst, sem, to, recv=None):
        cp = copy_to(src, dst, sem, to, recv)
        pl.when(cond)(cp.start)
        drains.append((cond, cp))
        return cp

    gap_all[g] = gaps[...]
    gap_sems = [slot() for _ in range(3)]
    gap_copies = []
    for d in range(1, 4):
        o = (g + d) % 4
        gap_copies.append(
            send(gaps, gap_all.at[g], gap_sems[d - 1], device(x, z, yh, o // 2, o % 2))
        )

    def turn(i, j):
        start = pl.multiple_of((i * 4 + j) * 128, 128)
        bt[i, j] = basis[:, pl.ds(start, 128)].T

    loads[0].wait()
    loads[1].wait()
    for j in range(4):
        turn((x + 2) % 4, j)

    def block(axis, q, lo, width):
        rows = bt[q] if axis == "x" else bt[:, q]
        return jnp.dot(
            rows.reshape(512, NK), dens[:, lo : lo + width], preferred_element_type=F32
        )

    here = {"x": x, "z": z}
    sem1 = {}

    def first_start(b, axis):
        h = 0 if axis == "x" else 1
        me, lo = here[axis], b * W + h * H
        sems = [slot() for _ in range(6)]
        far, near = s1_far.at[b, h], s1_near.at[b, h]
        if b == 1 and axis == "x":
            loads[5].wait()
        if b == 0 and axis == "z":
            for n, d in enumerate((0, 1, 3)):
                loads[n + 2].wait()
                turn((x + d) % 4, (z + 2) % 4)
        value = block(axis, (me + 2) % 4, lo, H).astype(BF16)
        far[0] = value[:, :Q]
        far[1] = value[:, Q:]
        recv = s1_recv.at[b, h]
        copies = [
            send(far.at[0], recv.at[0], sems[0], along(axis, 1)),
            send(far.at[1], recv.at[1], sems[1], along(axis, 3)),
        ]
        sem1[b, axis] = (sems, copies)

    def near_part(b, axis):
        h = 0 if axis == "x" else 1
        me, lo = here[axis], b * W + h * H
        sems, copies = sem1[b, axis]
        near, recv = s1_near.at[b, h], s1_recv.at[b, h]
        value = block(axis, (me + 1) % 4, lo, H)
        near[1] = value[:, Q:].astype(BF16)
        copies.append(send(near.at[1], recv.at[3], sems[3], along(axis, 1)))
        own_f32[b, h, 0] = value[:, :Q]
        value = block(axis, (me + 3) % 4, lo, H)
        near[2] = value[:, :Q].astype(BF16)
        copies.append(send(near.at[2], recv.at[4], sems[4], along(axis, 3)))
        own_f32[b, h, 1] = value[:, Q:]

    def first_own(b, axis):
        h = 0 if axis == "x" else 1
        me, lo = here[axis], b * W + h * H
        s1_sum[b, h] = block(axis, me, lo, H)

    def first_forward(b, axis):
        h = 0 if axis == "x" else 1
        sems, copies = sem1[b, axis]
        near, recv = s1_near.at[b, h], s1_recv.at[b, h]
        copies[0].wait_recv()
        near[0] = (own_f32[b, h, 0] + recv[0].astype(F32)).astype(BF16)
        copies.append(send(near.at[0], recv.at[2], sems[2], along(axis, 1)))
        copies[1].wait_recv()
        near[3] = (own_f32[b, h, 1] + recv[1].astype(F32)).astype(BF16)
        copies.append(send(near.at[3], recv.at[5], sems[5], along(axis, 3)))

    def first_end(b, axis):
        h = 0 if axis == "x" else 1
        recv = s1_recv.at[b, h]
        for cp in sem1[b, axis][1][2:]:
            cp.wait_recv()
        total = s1_sum.at[b, h]
        total[:, :Q] = total[:, :Q] + recv[2].astype(F32) + recv[4].astype(F32)
        total[:, Q:] = total[:, Q:] + recv[3].astype(F32) + recv[5].astype(F32)

    sem2 = {}

    def second_start(b, axis):
        h = 0 if axis == "x" else 1
        other = "z" if axis == "x" else "x"
        me = here[other]
        sems = [slot() for _ in range(3)]
        copies = []
        for i, d in enumerate((2, 1, 3)):
            start = pl.multiple_of((me + d) % 4 * 128, 128)
            s2_send[b, h, i] = s1_sum[b, h, pl.ds(start, 128), :].astype(BF16)
            copies.append(
                send(s2_send.at[b, h, i], s2_recv.at[b, h, i], sems[i], along(other, d))
            )
        sem2[b, axis] = copies

    is_home = g == x
    is_source = is_home
    step = 1 - 2 * (g % 2)
    rel = (x - g + 4) % 4
    is_out1 = rel == (4 - step) % 4
    pair_to = device((g + step + 4) % 4, z, yh, yl, c)
    out1_to = device((g - step + 4) % 4, z, yh, yl, c)
    out2_to = device((g + 2) % 4, z, yh, yl, c)

    def split(b):
        return b == 0

    sem_y = {}

    def second_end(b, axis):
        h = 0 if axis == "x" else 1
        other = "z" if axis == "x" else "x"
        for cp in sem2[b, axis]:
            cp.wait_recv()
        start = pl.multiple_of(here[other] * 128, 128)
        total = s1_sum[b, h, pl.ds(start, 128), :]
        for i in range(3):
            total = total + s2_recv[b, h, i].astype(F32)
        t_own[b, h] = total
        theirs = pl.multiple_of((1 - yh) * 64, 64)
        y_send[b, h] = t_own[b, h, pl.ds(theirs, 64), :].astype(BF16)
        sem_y[b, h] = send(y_send.at[b, h], y_recv.at[b, h], slot(), beside(4))

    own_rows = pl.ds(pl.multiple_of(yh * 64, 64), 64)

    def rows_start(b):
        for h in range(2):
            sem_y[b, h].wait_recv()
            value = (t_own[b, h, own_rows, :] + y_recv[b, h].astype(F32)).astype(BF16)
            proj[:, b * W + h * H : b * W + (h + 1) * H] = value
            ib[b, g, h] = value
        other_home = device(x, z, 1 - yh, x // 2, x % 2)
        for h in range(2):
            cond = yl != yh if h == 1 and split(b) else None
            pair = (ib.at[b, g, h], jb.at[b, z, h, g, own_rows])
            if cond is None:
                send(*pair, slot(), other_home, recv=home_sem.at[b, h, g])
            else:
                send_if(cond, *pair, slot(), other_home, recv=home_sem.at[b, h, g])
        mine = ib.at[b, g]
        send_if(
            g != x, mine, mine, slot(), device(x, z, yh, x // 2, x % 2),
            recv=row_sem.at[b, (x - g + 4) % 4],
        )

    def rows_more(b):
        mine = ib.at[b, g]
        for d in range(1, 4):
            o = (g + d) % 4
            send_if(
                o != x, mine, mine, slot(), device(x, z, yh, o // 2, o % 2),
                recv=row_sem.at[b, d],
            )

    def rows_end(b):
        for d in range(1, 4):
            o = (g - d + 4) % 4
            copy_to(ib.at[b, o], ib.at[b, o], 0, along("x", 1), recv=row_sem.at[b, d]).wait_recv()

    def weigh(b):
        if b == 0:
            for cp in gap_copies:
                cp.wait_recv()
        column = lax.broadcasted_iota(jnp.int32, (NFREQ, W), 0)
        square = jnp.zeros((NFREQ, W), F32)
        for k in range(NFREQ):
            square = jnp.where(column == k, freq[k] * freq[k], square)
        for gg in range(4):
            gap = gap_all[gg, :, b * W : (b + 1) * W]
            value = (-4.0 / PAIRS) * gap / (gap * gap + square)
            for h in range(2):
                wts[b, h, :, gg * H : (gg + 1) * H] = value[:, h * H : (h + 1) * H]

    def scale(b):
        pl.when(jnp.logical_not(is_home))(lambda: rows_end(b))
        for h in range(2):
            for gg in range(4):
                sl = slice(gg * H, (gg + 1) * H)
                rows = ib[b, gg, h].astype(F32)

                def at(k, _, h=h, sl=sl, rows=rows):
                    start = pl.multiple_of(k * 64, 64)
                    scaled[b, h, pl.ds(start, 64), sl] = (
                        wts[b, h, pl.ds(k, 1), sl] * rows
                    ).astype(BF16)
                    return 0

                lax.fori_loop(0, NFREQ, at, 0)

    sem_g = {}
    zn = [z, (z + 3) % 4, (z + 1) % 4, (z + 2) % 4]

    def wait_in(dst, sem, to):
        copy_to(dst, dst, sem, to).wait_recv()

    def part(b, zz, h):
        if h == 1 and split(b):
            return jb.at[b, zz, 1, pl.ds(2 * yh, 2)]
        return jb.at[b, zz, h]

    def half(b, zz, h, n):
        if h == 1 and split(b):
            return jb.at[b, zz, 1, pl.ds(2 * yh + n, 1)]
        return jb.at[b, zz, h, pl.ds(2 * n, 2)]

    def pieces(b, zz, h):
        if h == 1 and split(b):
            return [part(b, zz, h)]
        return [half(b, zz, h, n) for n in range(2)]

    def gather1(b):
        ss = {name + str(h): slot() for name in ("a0", "a1", "b0", "b1", "c", "d") for h in range(2)}
        for n in range(2):
            ss["x1", n] = slot()
            ss["x1o", n] = slot()
        for i in range(4):
            for n in range(1 if split(b) else 2):
                ss["x2", i, n] = slot()
                ss["x2o", i, n] = slot()
            if split(b):
                ss["y2", i] = slot()
        sem_g[b] = ss
        pl.when(is_home)(lambda: rows_end(b))
        for h in range(2):

            @pl.when(is_home)
            def _(h=h):
                groups = [2 * yh, 2 * yh + 1] if h == 1 and split(b) else range(4)
                for gg in groups:
                    jb[b, z, h, gg, own_rows, :] = ib[b, gg, h]
                for gg in groups:
                    block = jb.at[b, z, h, gg, own_rows]
                    copy_to(block, block, 0, along("x", 1), recv=home_sem.at[b, h, gg]).wait_recv()

            if h == 0:
                for n, piece in enumerate(pieces(b, z, 0)):
                    send_if(is_source, piece, piece, ss["x1", n], out1_to)
                    send_if(
                        is_source, piece, piece, ss["x1o", n], pair_to,
                        recv=recv_sem.at[ss["x1", n]],
                    )
            else:
                ring_start(b, 1, is_source)

    def ring_start(b, h, cond):
        ss = sem_g[b]
        for n in range(2):
            up, down = half(b, z, h, n), half(b, z, h, 1 - n)
            one = (up, up, ss[f"a{n}{h}"], along("z", 1))
            two = (down, down, ss[f"b{1 - n}{h}"], along("z", 3))
            for args in (one, two):
                if cond is None:
                    send(*args)
                else:
                    send_if(cond, *args)

    def gather2(b):
        ss = sem_g[b]
        for n, piece in enumerate(pieces(b, z, 0)):

            @pl.when(jnp.logical_not(is_source))
            def _(n=n, piece=piece):
                wait_in(piece, ss["x1", n], along("x", 1))

            fwd = copy_to(piece, piece, ss["x1", n], out2_to)
            pl.when(is_out1)(fwd.start)
            drains.append((is_out1, fwd))
        ring_start(b, 0, None)
        spread2(b, 0)

    def spread2(b, i, which=None):
        ss = sem_g[b]
        for n, piece in enumerate(pieces(b, zn[i], 1)):
            if which is None or n == which:
                send_if(is_source, piece, piece, ss["x2", i, n], out1_to)
                send_if(
                    is_source, piece, piece, ss["x2o", i, n], pair_to,
                    recv=recv_sem.at[ss["x2", i, n]],
                )

    def pass2(b, i):
        ss = sem_g[b]
        for n, piece in enumerate(pieces(b, zn[i], 1)):

            @pl.when(jnp.logical_not(is_source))
            def _(n=n, piece=piece):
                wait_in(piece, ss["x2", i, n], along("x", 1))

            fwd = copy_to(piece, piece, ss["x2", i, n], out2_to)
            pl.when(is_out1)(fwd.start)
            drains.append((is_out1, fwd))
        if split(b):
            send(piece, piece, ss["y2", i], beside(4))

    def across_end(b, i):
        wait_in(jb.at[b, zn[i], 1, pl.ds(2 - 2 * yh, 2)], sem_g[b]["y2", i], beside(4))

    def under(cond, go):
        if cond is None:
            go()
        else:
            pl.when(cond)(go)

    def ring_mid(b, h, cond):
        ss = sem_g[b]
        lower, upper = half(b, zn[1], h, 0), half(b, zn[2], h, 1)
        for ref, name, on, d in ((lower, "a0", "c", 1), (upper, "b1", "d", 3)):
            under(cond, lambda ref=ref, name=name: wait_in(ref, ss[f"{name}{h}"], along("z", 1)))
            if cond is None:
                send(ref, ref, ss[f"{on}{h}"], along("z", d))
            else:
                send_if(cond, ref, ref, ss[f"{on}{h}"], along("z", d))
        for i, n, name in ((1, 1, "a1"), (2, 0, "b0")):
            ref = half(b, zn[i], h, n)
            under(cond, lambda ref=ref, name=name: wait_in(ref, ss[f"{name}{h}"], along("z", 1)))

    def ring_end(b, h, cond, after=None):
        ss = sem_g[b]
        for n, name in enumerate("cd"):
            ref = half(b, zn[3], h, n)
            under(cond, lambda ref=ref, name=name: wait_in(ref, ss[f"{name}{h}"], along("z", 1)))
            if after is not None:
                after(n)

    def gather3(b):
        ring_mid(b, 1, is_source)
        spread2(b, 1)
        spread2(b, 2)
        ring_mid(b, 0, None)
        pass2(b, 0)

    def gather4(b):
        if split(b):
            ring_end(b, 1, is_source)
            spread2(b, 3)
        else:
            ring_end(b, 1, is_source, lambda n: spread2(b, 3, n))
        pass2(b, 1)
        pass2(b, 2)

    def gather5(b):
        ring_end(b, 0, None)
        pass2(b, 3)

    def multiply(b, h, which, first=False):
        if h == 1 and split(b):
            for i in which:
                across_end(b, i)
        rows = jnp.concatenate(
            [
                jnp.concatenate([jb[b, zn[i], h, gg] for gg in range(4)], axis=1)
                for i in which
            ],
            axis=0,
        )
        value = lax.dot_general(
            scaled[b, h], rows, (((1,), (1,)), ((), ())), preferred_element_type=F32
        )
        for n, i in enumerate(which):
            col = pl.ds(pl.multiple_of(zn[i] * 128, 128), 128)
            share = value[:, n * 128 : (n + 1) * 128]
            if first:
                pol[:, col] = share
            else:
                pol[:, col] += share

    first_start(0, 'x')
    first_start(0, 'z')
    for d in (0, 1, 3):
        for e in (0, 1, 3):
            turn((x + d) % 4, (z + e) % 4)
    near_part(0, 'x')
    near_part(0, 'z')
    first_start(1, 'x')
    first_start(1, 'z')
    first_own(0, 'x')
    first_own(0, 'z')
    first_forward(0, 'x')
    first_forward(0, 'z')
    near_part(1, 'x')
    near_part(1, 'z')
    first_own(1, 'x')
    first_own(1, 'z')
    first_end(0, 'x')
    first_end(0, 'z')
    second_start(0, 'x')
    second_start(0, 'z')
    first_forward(1, 'x')
    first_forward(1, 'z')
    weigh(0)
    weigh(1)
    second_end(0, 'x')
    second_end(0, 'z')
    first_end(1, 'x')
    first_end(1, 'z')
    second_start(1, 'x')
    second_start(1, 'z')
    rows_start(0)
    second_end(1, 'x')
    second_end(1, 'z')
    gather1(0)
    rows_start(1)
    gather2(0)
    rows_more(0)
    gather1(1)
    gather3(0)
    gather2(1)
    rows_more(1)
    gather4(0)
    scale(0)
    gather3(1)
    multiply(0, 0, (0, 1), first=True)
    gather5(0)
    scale(1)
    multiply(0, 0, (2, 3), first=True)
    gather4(1)
    multiply(0, 1, (0, 1))
    multiply(0, 1, (2, 3))
    multiply(1, 0, (0, 1))
    multiply(1, 1, (0, 1))
    gather5(1)
    multiply(1, 0, (2, 3))
    multiply(1, 1, (2, 3))
    for cond, cp in drains:
        if cond is None:
            cp.wait_send()
        else:
            pl.when(cond)(cp.wait_send)


def on_device(basis_set, densities, pair_gaps, frequencies):
    any_, vmem = pl.BlockSpec(memory_space=pl.ANY), pl.BlockSpec(memory_space=pltpu.VMEM)
    pol, proj = pl.pallas_call(
        kernel,
        out_shape=(
            pltpu.VMEM((NFREQ * 64, 512), F32),
            pltpu.VMEM((64, NP), BF16),
        ),
        in_specs=[any_, any_, vmem, pl.BlockSpec(memory_space=pltpu.SMEM)],
        out_specs=(vmem, vmem),
        scratch_shapes=[
            pltpu.VMEM((NK, NB), BF16),
            pltpu.VMEM((NK, NP), BF16),
            pltpu.VMEM((4, 4, 128, NK), BF16),
            pltpu.VMEM((NBT, 2, 2, 512, Q), F32),
            pltpu.VMEM((NBT, 2, 6, 512, Q), BF16),
            pltpu.VMEM((NBT, 2, 2, 512, Q), BF16),
            pltpu.VMEM((NBT, 2, 4, 512, Q), BF16),
            pltpu.VMEM((NBT, 2, 512, H), F32),
            pltpu.VMEM((NBT, 2, 3, 128, H), BF16),
            pltpu.VMEM((NBT, 2, 3, 128, H), BF16),
            pltpu.VMEM((NBT, 2, 128, H), F32),
            pltpu.VMEM((NBT, 2, 64, H), BF16),
            pltpu.VMEM((NBT, 2, 64, H), BF16),
            pltpu.VMEM((NBT, 4, 2, 64, H), BF16),
            pltpu.VMEM((4, 1, NP), F32),
            pltpu.VMEM((NBT, 2, NFREQ, 2 * W), F32),
            pltpu.VMEM((NBT, 2, NFREQ * 64, 2 * W), BF16),
            pltpu.VMEM((NBT, 4, 2, 4, 128, H), BF16),
            pltpu.SemaphoreType.DMA((6,)),
            pltpu.SemaphoreType.DMA((NSEM,)),
            pltpu.SemaphoreType.DMA((NSEM,)),
            pltpu.SemaphoreType.DMA((NBT, 2, 4)),
            pltpu.SemaphoreType.DMA((NBT, 4)),
        ],
        compiler_params=pltpu.CompilerParams(
            collective_id=0, has_side_effects=True, vmem_limit_bytes=56 * 2**20
        ),
    )(basis_set, densities, pair_gaps.reshape(1, NP), frequencies)
    return pol.reshape(NFREQ, 64, 512), proj


def solution(mesh):
    in_specs = (P("pw", None), P("pw", "band"), P("band"), P())
    out_specs = (P(None, "pw", "band"), P("pw", "band"))
    return jax.shard_map(
        on_device, mesh=mesh, in_specs=in_specs, out_specs=out_specs, check_vma=False
    )
```

```python
import functools

import jax
import jax.numpy as jnp
from jax import lax
from jax.experimental import pallas as pl
from jax.experimental.pallas import tpu as pltpu
from jax.sharding import PartitionSpec as P

MESH = pl.DeviceIdType.MESH
F32, BF16 = jnp.float32, jnp.bfloat16

NK = 768
NB = 2048
NP = 1024
NFREQ = 16
PAIRS = 4096
NBT = 4
W = NP // NBT
H = W // 2
HALF = 256
NSEM = 3 + NBT * 32


def device(x, z, yh, yl, c):
    return ((x * 4 + z) * 2 + yh, yl * 2 + c)


def kernel(
    basis_hbm, dens_hbm, gaps, freq,
    pol, proj,
    basis, dens, bt,
    own_f32, s1_recv, s1_far, s1_near, s1_sum,
    s2_send, s2_recv,
    t_own, y_send, y_recv,
    ib, gap_all, wts, scaled, jb,
    load_sem, send_sem, recv_sem, home_sem, row_sem,
):
    pw, g = lax.axis_index("pw"), lax.axis_index("band")
    x, z, yh = pw // 8, (pw // 2) % 4, pw % 2
    yl, c = g // 2, g % 2
    me8 = yh * 4 + g

    def fetch(src, dst, cols, n):
        return pltpu.make_async_copy(src.at[:, cols], dst.at[:, cols], load_sem.at[n])

    loads = [fetch(dens_hbm, dens, pl.ds(0, W), 0)]
    for n, d in enumerate((2, 0, 1, 3)):
        cols = pl.ds(pl.multiple_of((x + d) % 4 * 512, 512), 512)
        loads.append(fetch(basis_hbm, basis, cols, n + 1))
    loads.append(fetch(dens_hbm, dens, pl.ds(W, NP - W), 5))
    for load in loads:
        load.start()

    def along(axis, d):
        if axis == "x":
            return device((x + d) % 4, z, yh, yl, c)
        return device(x, (z + d) % 4, yh, yl, c)

    def beside(d):
        o = (me8 + d) % 8
        return device(x, z, o // 4, (o % 4) // 2, o % 2)

    barrier = pltpu.get_barrier_semaphore()
    peers = [along(a, d) for a in "xz" for d in (1, 2, 3)] + [beside(d) for d in range(1, 8)]
    for peer in peers:
        pl.semaphore_signal(barrier, inc=1, device_id=peer, device_id_type=MESH)
    pl.semaphore_wait(barrier, len(peers))

    drains = []
    count = [0]

    def slot():
        count[0] += 1
        assert count[0] <= NSEM
        return count[0] - 1

    def copy_to(src, dst, sem, to, recv=None):
        return pltpu.make_async_remote_copy(
            src_ref=src, dst_ref=dst, send_sem=send_sem.at[0],
            recv_sem=recv_sem.at[sem] if recv is None else recv,
            device_id=to, device_id_type=MESH,
        )

    def send(src, dst, sem, to, recv=None):
        cp = copy_to(src, dst, sem, to, recv)
        cp.start()
        drains.append((None, cp))
        return cp

    def send_if(cond, src, dst, sem, to, recv=None):
        cp = copy_to(src, dst, sem, to, recv)
        pl.when(cond)(cp.start)
        drains.append((cond, cp))
        return cp

    gap_all[g] = gaps[...]
    gap_sems = [slot() for _ in range(3)]
    gap_copies = []
    for d in range(1, 4):
        o = (g + d) % 4
        gap_copies.append(
            send(gaps, gap_all.at[g], gap_sems[d - 1], device(x, z, yh, o // 2, o % 2))
        )

    def turn(i, j):
        start = pl.multiple_of((i * 4 + j) * 128, 128)
        bt[i, j] = basis[:, pl.ds(start, 128)].T

    loads[0].wait()
    loads[1].wait()
    for j in range(4):
        turn((x + 2) % 4, j)

    def block(axis, q, lo, width):
        rows = bt[q] if axis == "x" else bt[:, q]
        return jnp.dot(
            rows.reshape(512, NK), dens[:, lo : lo + width], preferred_element_type=F32
        )

    here = {"x": x, "z": z}
    sem1 = {}

    def first_start(b, axis):
        h = 0 if axis == "x" else 1
        me, lo = here[axis], b * W + h * H
        sems = [slot() for _ in range(3)]
        far, near = s1_far.at[b, h], s1_near.at[b, h]
        if b == 1 and axis == "x":
            loads[5].wait()
        if b == 0 and axis == "z":
            for n, d in enumerate((0, 1, 3)):
                loads[n + 2].wait()
                turn((x + d) % 4, (z + 2) % 4)
        value = block(axis, (me + 2) % 4, lo, H).astype(BF16)
        far[0] = value[:HALF]
        far[1] = value[HALF:]
        recv = s1_recv.at[b, h]
        copies = [
            send(far.at[0], recv.at[0], sems[0], along(axis, 1)),
            send(far.at[1], recv.at[1], sems[1], along(axis, 3)),
        ]
        sem1[b, axis] = (sems, copies)

    def near_part(b, axis):
        h = 0 if axis == "x" else 1
        me, lo = here[axis], b * W + h * H
        sems, copies = sem1[b, axis]
        near, recv = s1_near.at[b, h], s1_recv.at[b, h]
        value = block(axis, (me + 1) % 4, lo, H)
        near[1] = value[HALF:].astype(BF16)
        copies.append(send(near.at[1], recv.at[3], sems[2], along(axis, 1)))
        own_f32[b, h, 0] = value[:HALF]
        value = block(axis, (me + 3) % 4, lo, H)
        near[2] = value[:HALF].astype(BF16)
        copies.append(send(near.at[2], recv.at[4], sems[2], along(axis, 3)))
        own_f32[b, h, 1] = value[HALF:]

    def first_own(b, axis):
        h = 0 if axis == "x" else 1
        me, lo = here[axis], b * W + h * H
        s1_sum[b, h] = block(axis, me, lo, H)

    def first_forward(b, axis):
        h = 0 if axis == "x" else 1
        sems, copies = sem1[b, axis]
        near, recv = s1_near.at[b, h], s1_recv.at[b, h]
        copies[0].wait_recv()
        near[0] = (own_f32[b, h, 0] + recv[0].astype(F32)).astype(BF16)
        copies.append(send(near.at[0], recv.at[2], sems[2], along(axis, 1)))
        copies[1].wait_recv()
        near[3] = (own_f32[b, h, 1] + recv[1].astype(F32)).astype(BF16)
        copies.append(send(near.at[3], recv.at[5], sems[2], along(axis, 3)))

    def first_end(b, axis):
        h = 0 if axis == "x" else 1
        recv = s1_recv.at[b, h]
        last = recv.at[pl.ds(2, 4)]
        copy_to(last, last, sem1[b, axis][0][2], along(axis, 1)).wait_recv()
        total = s1_sum.at[b, h]
        total[:HALF] = total[:HALF] + recv[2].astype(F32) + recv[4].astype(F32)
        total[HALF:] = total[HALF:] + recv[3].astype(F32) + recv[5].astype(F32)

    sem2 = {}

    def second_start(b, axis):
        h = 0 if axis == "x" else 1
        other = "z" if axis == "x" else "x"
        me = here[other]
        sem = slot()
        for i, d in enumerate((2, 1, 3)):
            start = pl.multiple_of((me + d) % 4 * 128, 128)
            s2_send[b, h, i] = s1_sum[b, h, pl.ds(start, 128), :].astype(BF16)
            send(s2_send.at[b, h, i], s2_recv.at[b, h, i], sem, along(other, d))
        sem2[b, axis] = sem

    is_home = g == x
    is_source = is_home
    step = 1 - 2 * (g % 2)
    rel = (x - g + 4) % 4
    is_out1 = rel == (4 - step) % 4
    pair_to = device((g + step + 4) % 4, z, yh, yl, c)
    out1_to = device((g - step + 4) % 4, z, yh, yl, c)
    out2_to = device((g + 2) % 4, z, yh, yl, c)

    def split(b):
        return b in (1, 2)

    sem_y = {}

    def second_end(b, axis):
        h = 0 if axis == "x" else 1
        other = "z" if axis == "x" else "x"
        every = s2_recv.at[b, h]
        copy_to(every, every, sem2[b, axis], along(other, 1)).wait_recv()
        start = pl.multiple_of(here[other] * 128, 128)
        total = s1_sum[b, h, pl.ds(start, 128), :]
        for i in range(3):
            total = total + s2_recv[b, h, i].astype(F32)
        t_own[b, h] = total
        theirs = pl.multiple_of((1 - yh) * 64, 64)
        y_send[b, h] = t_own[b, h, pl.ds(theirs, 64), :].astype(BF16)
        sem_y[b, h] = send(y_send.at[b, h], y_recv.at[b, h], slot(), beside(4))

    own_rows = pl.ds(pl.multiple_of(yh * 64, 64), 64)

    def rows_start(b):
        for h in range(2):
            sem_y[b, h].wait_recv()
            value = (t_own[b, h, own_rows, :] + y_recv[b, h].astype(F32)).astype(BF16)
            proj[:, b * W + h * H : b * W + (h + 1) * H] = value
            ib[b, g, h] = value
        other_home = device(x, z, 1 - yh, x // 2, x % 2)
        for h in range(2):
            cond = yl != yh if h == 1 and split(b) else None
            pair = (ib.at[b, g, h], jb.at[b, z, h, g, own_rows])
            if cond is None:
                send(*pair, 0, other_home, recv=home_sem.at[b, h])
            else:
                send_if(cond, *pair, 0, other_home, recv=home_sem.at[b, h])
        mine = ib.at[b, g]
        send_if(
            g != x, mine, mine, 0, device(x, z, yh, x // 2, x % 2),
            recv=row_sem.at[b],
        )

    def rows_more(b):
        mine = ib.at[b, g]
        for d in range(1, 4):
            o = (g + d) % 4
            send_if(
                o != x, mine, mine, 0, device(x, z, yh, o // 2, o % 2),
                recv=row_sem.at[b],
            )

    def rows_end(b):
        three = ib.at[b, pl.ds(0, 3)]
        copy_to(three, three, 0, along("x", 1), recv=row_sem.at[b]).wait_recv()

    def weigh(b):
        if b == 0:
            for cp in gap_copies:
                cp.wait_recv()
        column = lax.broadcasted_iota(jnp.int32, (NFREQ, W), 0)
        square = jnp.zeros((NFREQ, W), F32)
        for k in range(NFREQ):
            square = jnp.where(column == k, freq[k] * freq[k], square)
        for gg in range(4):
            gap = gap_all[gg, :, b * W : (b + 1) * W]
            value = (-4.0 / PAIRS) * gap / (gap * gap + square)
            for h in range(2):
                wts[b, h, :, gg * H : (gg + 1) * H] = value[:, h * H : (h + 1) * H]

    def scale(b):
        pl.when(jnp.logical_not(is_home))(lambda: rows_end(b))
        for h in range(2):
            rows = jnp.concatenate([ib[b, gg, h] for gg in range(4)], axis=1).astype(F32)

            def at(k, _, h=h, rows=rows):
                start = pl.multiple_of(k * 64, 64)
                scaled[b, h, pl.ds(start, 64), :] = (
                    wts[b, h, pl.ds(k, 1), :] * rows
                ).astype(BF16)
                return 0

            lax.fori_loop(0, NFREQ, at, 0)

    sem_g = {}
    zn = [z, (z + 3) % 4, (z + 1) % 4, (z + 2) % 4]

    def wait_in(dst, sem, to):
        copy_to(dst, dst, sem, to).wait_recv()

    def part(b, zz, h):
        if h == 1 and split(b):
            return jb.at[b, zz, 1, pl.ds(2 * yh, 2)]
        return jb.at[b, zz, h]

    def half(b, zz, h, n):
        if h == 1 and split(b):
            return jb.at[b, zz, 1, pl.ds(2 * yh + n, 1)]
        return jb.at[b, zz, h, pl.ds(2 * n, 2)]

    def pieces(b, zz, h):
        if h == 1 and split(b):
            return [part(b, zz, h)]
        return [half(b, zz, h, n) for n in range(2)]

    def gather1(b):
        ss = {name + str(h): slot() for name in ("a0", "ab", "b1", "c", "d") for h in range(2)}
        for n in range(2):
            ss["x1", n] = slot()
        for i in range(4):
            for n in range(1 if split(b) else 2):
                ss["x2", i, n] = slot()
            if split(b):
                ss["y2", i] = slot()
        sem_g[b] = ss
        pl.when(is_home)(lambda: rows_end(b))
        for h in range(2):

            @pl.when(is_home)
            def _(h=h):
                groups = [2 * yh, 2 * yh + 1] if h == 1 and split(b) else range(4)
                for gg in groups:
                    jb[b, z, h, gg, own_rows, :] = ib[b, gg, h]
                block = jb.at[b, z, h, pl.ds(0, len(groups)), own_rows]
                copy_to(block, block, 0, along("x", 1), recv=home_sem.at[b, h]).wait_recv()

            if h == 0:
                for n, piece in enumerate(pieces(b, z, 0)):
                    send_if(is_source, piece, piece, ss["x1", n], out1_to)
                    send_if(
                        is_source, piece, piece, ss["x1", n], pair_to
                    )
            else:
                ring_start(b, 1, is_source)

    def ring_start(b, h, cond):
        ss = sem_g[b]
        for n in range(2):
            up, down = half(b, z, h, n), half(b, z, h, 1 - n)
            one = (up, up, ss[("a0", "ab")[n] + str(h)], along("z", 1))
            two = (down, down, ss[("b1", "ab")[n] + str(h)], along("z", 3))
            for args in (one, two):
                if cond is None:
                    send(*args)
                else:
                    send_if(cond, *args)

    def gather2(b):
        ss = sem_g[b]
        for n, piece in enumerate(pieces(b, z, 0)):

            @pl.when(jnp.logical_not(is_source))
            def _(n=n, piece=piece):
                wait_in(piece, ss["x1", n], along("x", 1))

            fwd = copy_to(piece, piece, ss["x1", n], out2_to)
            pl.when(is_out1)(fwd.start)
            drains.append((is_out1, fwd))
        ring_start(b, 0, None)
        spread2(b, 0)

    def spread2(b, i, which=None):
        ss = sem_g[b]
        for n, piece in enumerate(pieces(b, zn[i], 1)):
            if which is None or n == which:
                send_if(is_source, piece, piece, ss["x2", i, n], out1_to)
                send_if(
                    is_source, piece, piece, ss["x2", i, n], pair_to
                )

    def pass2(b, i):
        ss = sem_g[b]
        for n, piece in enumerate(pieces(b, zn[i], 1)):

            @pl.when(jnp.logical_not(is_source))
            def _(n=n, piece=piece):
                wait_in(piece, ss["x2", i, n], along("x", 1))

            fwd = copy_to(piece, piece, ss["x2", i, n], out2_to)
            pl.when(is_out1)(fwd.start)
            drains.append((is_out1, fwd))
        if split(b):
            send(piece, piece, ss["y2", i], beside(4))

    def across_end(b, i):
        wait_in(jb.at[b, zn[i], 1, pl.ds(2 - 2 * yh, 2)], sem_g[b]["y2", i], beside(4))

    def under(cond, go):
        if cond is None:
            go()
        else:
            pl.when(cond)(go)

    def ring_mid(b, h, cond):
        ss = sem_g[b]
        lower, upper = half(b, zn[1], h, 0), half(b, zn[2], h, 1)
        for ref, name, on, d in ((lower, "a0", "c", 1), (upper, "b1", "d", 3)):
            under(cond, lambda ref=ref, name=name: wait_in(ref, ss[f"{name}{h}"], along("z", 1)))
            if cond is None:
                send(ref, ref, ss[f"{on}{h}"], along("z", d))
            else:
                send_if(cond, ref, ref, ss[f"{on}{h}"], along("z", d))
        under(cond, lambda: wait_in(part(b, zn[1], h), ss[f"ab{h}"], along("z", 1)))

    def ring_end(b, h, cond, after=None):
        ss = sem_g[b]
        for n, name in enumerate("cd"):
            ref = half(b, zn[3], h, n)
            under(cond, lambda ref=ref, name=name: wait_in(ref, ss[f"{name}{h}"], along("z", 1)))
            if after is not None:
                after(n)

    def gather3(b):
        ring_mid(b, 1, is_source)
        spread2(b, 1)
        spread2(b, 2)
        ring_mid(b, 0, None)
        pass2(b, 0)

    def gather4(b):
        if split(b):
            ring_end(b, 1, is_source)
            spread2(b, 3)
        else:
            ring_end(b, 1, is_source, lambda n: spread2(b, 3, n))
        pass2(b, 1)
        pass2(b, 2)

    def gather5(b):
        ring_end(b, 0, None)
        pass2(b, 3)

    def multiply(b, h, which, first=False):
        if h == 1 and split(b):
            for i in which:
                across_end(b, i)
        rows = jnp.concatenate(
            [
                jnp.concatenate([jb[b, zn[i], h, gg] for gg in range(4)], axis=1)
                for i in which
            ],
            axis=0,
        )
        value = lax.dot_general(
            scaled[b, h], rows, (((1,), (1,)), ((), ())), preferred_element_type=F32
        )
        for n, i in enumerate(which):
            col = pl.ds(pl.multiple_of(zn[i] * 128, 128), 128)
            share = value[:, n * 128 : (n + 1) * 128]
            if first:
                pol[:, col] = share
            else:
                pol[:, col] += share

    first_start(0, 'x')
    first_start(0, 'z')
    for d in (0, 1, 3):
        for e in (0, 1, 3):
            turn((x + d) % 4, (z + e) % 4)
    near_part(0, 'x')
    near_part(0, 'z')
    first_own(0, 'x')
    first_own(0, 'z')
    first_forward(0, 'x')
    first_forward(0, 'z')
    first_start(1, 'x')
    first_start(1, 'z')
    near_part(1, 'x')
    near_part(1, 'z')
    first_own(1, 'x')
    first_own(1, 'z')
    first_end(0, 'x')
    first_end(0, 'z')
    second_start(0, 'x')
    second_start(0, 'z')
    weigh(0)
    first_forward(1, 'x')
    first_forward(1, 'z')
    first_start(2, 'x')
    first_start(2, 'z')
    near_part(2, 'x')
    near_part(2, 'z')
    first_own(2, 'x')
    first_own(2, 'z')
    second_end(0, 'x')
    second_end(0, 'z')
    first_end(1, 'x')
    first_end(1, 'z')
    second_start(1, 'x')
    second_start(1, 'z')
    weigh(1)
    first_forward(2, 'x')
    first_forward(2, 'z')
    first_start(3, 'x')
    first_start(3, 'z')
    near_part(3, 'x')
    near_part(3, 'z')
    first_own(3, 'x')
    first_own(3, 'z')
    rows_start(0)
    second_end(1, 'x')
    second_end(1, 'z')
    first_end(2, 'x')
    first_end(2, 'z')
    second_start(2, 'x')
    second_start(2, 'z')
    weigh(2)
    first_forward(3, 'x')
    first_forward(3, 'z')
    gather1(0)
    rows_start(1)
    second_end(2, 'x')
    second_end(2, 'z')
    first_end(3, 'x')
    first_end(3, 'z')
    second_start(3, 'x')
    second_start(3, 'z')
    weigh(3)
    gather2(0)
    rows_more(0)
    rows_start(2)
    gather1(1)
    second_end(3, 'x')
    second_end(3, 'z')
    gather3(0)
    scale(0)
    gather2(1)
    rows_more(1)
    rows_start(3)
    gather4(0)
    gather1(2)
    multiply(0, 0, (0, 1), first=True)
    gather3(1)
    gather5(0)
    scale(1)
    gather2(2)
    multiply(0, 0, (2, 3), first=True)
    multiply(0, 1, (0, 1))
    rows_more(2)
    gather4(1)
    gather1(3)
    multiply(1, 0, (0, 1))
    gather3(2)
    multiply(0, 1, (2, 3))
    gather5(1)
    scale(2)
    gather2(3)
    multiply(1, 0, (2, 3))
    multiply(1, 1, (0, 1))
    rows_more(3)
    gather4(2)
    multiply(2, 0, (0, 1))
    gather3(3)
    multiply(1, 1, (2, 3))
    gather5(2)
    scale(3)
    multiply(2, 0, (2, 3))
    multiply(2, 1, (0, 1))
    gather4(3)
    multiply(3, 0, (0, 1))
    multiply(2, 1, (2, 3))
    gather5(3)
    multiply(3, 0, (2, 3))
    multiply(3, 1, (0, 1))
    multiply(3, 1, (2, 3))
    for cond, cp in drains:
        if cond is None:
            cp.wait_send()
        else:
            pl.when(cond)(cp.wait_send)


def on_device(basis_set, densities, pair_gaps, frequencies):
    any_, vmem = pl.BlockSpec(memory_space=pl.ANY), pl.BlockSpec(memory_space=pltpu.VMEM)
    pol, proj = pl.pallas_call(
        kernel,
        out_shape=(
            pltpu.VMEM((NFREQ * 64, 512), F32),
            pltpu.VMEM((64, NP), BF16),
        ),
        in_specs=[any_, any_, vmem, pl.BlockSpec(memory_space=pltpu.SMEM)],
        out_specs=(vmem, vmem),
        scratch_shapes=[
            pltpu.VMEM((NK, NB), BF16),
            pltpu.VMEM((NK, NP), BF16),
            pltpu.VMEM((4, 4, 128, NK), BF16),
            pltpu.VMEM((NBT, 2, 2, HALF, H), F32),
            pltpu.VMEM((NBT, 2, 6, HALF, H), BF16),
            pltpu.VMEM((NBT, 2, 2, HALF, H), BF16),
            pltpu.VMEM((NBT, 2, 4, HALF, H), BF16),
            pltpu.VMEM((NBT, 2, 512, H), F32),
            pltpu.VMEM((NBT, 2, 3, 128, H), BF16),
            pltpu.VMEM((NBT, 2, 3, 128, H), BF16),
            pltpu.VMEM((NBT, 2, 128, H), F32),
            pltpu.VMEM((NBT, 2, 64, H), BF16),
            pltpu.VMEM((NBT, 2, 64, H), BF16),
            pltpu.VMEM((NBT, 4, 2, 64, H), BF16),
            pltpu.VMEM((4, 1, NP), F32),
            pltpu.VMEM((NBT, 2, NFREQ, 2 * W), F32),
            pltpu.VMEM((NBT, 2, NFREQ * 64, 2 * W), BF16),
            pltpu.VMEM((NBT, 4, 2, 4, 128, H), BF16),
            pltpu.SemaphoreType.DMA((6,)),
            pltpu.SemaphoreType.DMA((1,)),
            pltpu.SemaphoreType.DMA((NSEM,)),
            pltpu.SemaphoreType.DMA((NBT, 2)),
            pltpu.SemaphoreType.DMA((NBT,)),
        ],
        compiler_params=pltpu.CompilerParams(
            collective_id=0, has_side_effects=True, vmem_limit_bytes=56 * 2**20
        ),
    )(basis_set, densities, pair_gaps.reshape(1, NP), frequencies)
    return pol.reshape(NFREQ, 64, 512), proj


def solution(mesh):
    in_specs = (P("pw", None), P("pw", "band"), P("band"), P())
    out_specs = (P(None, "pw", "band"), P("pw", "band"))
    return jax.shard_map(
        on_device, mesh=mesh, in_specs=in_specs, out_specs=out_specs, check_vma=False
    )
```

```python
import functools

import jax
import jax.numpy as jnp
from jax import lax
from jax.experimental import pallas as pl
from jax.experimental.pallas import tpu as pltpu
from jax.sharding import PartitionSpec as P

MESH = pl.DeviceIdType.MESH
F32, BF16 = jnp.float32, jnp.bfloat16

NK = 768
NB = 2048
NP = 1024
NFREQ = 16
PAIRS = 4096
NBT = 4
W = NP // NBT
H = W // 2
HALF = 256
NSEM = 3 + NBT * 32


def device(x, z, yh, yl, c):
    return ((x * 4 + z) * 2 + yh, yl * 2 + c)


def kernel(
    basis_hbm, dens_hbm, gaps, freq,
    pol, proj,
    basis, dens, bt,
    own_f32, s1_recv, s1_far, s1_near, s1_sum,
    s2_send, s2_recv,
    t_own, y_send, y_recv,
    ib, gap_all, wts, scaled, jb,
    load_sem, send_sem, recv_sem, home_sem, row_sem,
):
    pw, g = lax.axis_index("pw"), lax.axis_index("band")
    x, z, yh = pw // 8, (pw // 2) % 4, pw % 2
    yl, c = g // 2, g % 2
    me8 = yh * 4 + g

    def fetch(src, dst, cols, n):
        return pltpu.make_async_copy(src.at[:, cols], dst.at[:, cols], load_sem.at[n])

    loads = [fetch(dens_hbm, dens, pl.ds(0, W), 0)]
    for n, d in enumerate((2, 0, 1, 3)):
        cols = pl.ds(pl.multiple_of((x + d) % 4 * 512, 512), 512)
        loads.append(fetch(basis_hbm, basis, cols, n + 1))
    loads.append(fetch(dens_hbm, dens, pl.ds(W, NP - W), 5))
    for load in loads:
        load.start()

    def along(axis, d):
        if axis == "x":
            return device((x + d) % 4, z, yh, yl, c)
        return device(x, (z + d) % 4, yh, yl, c)

    def beside(d):
        o = (me8 + d) % 8
        return device(x, z, o // 4, (o % 4) // 2, o % 2)

    barrier = pltpu.get_barrier_semaphore()
    peers = [along(a, d) for a in "xz" for d in (1, 2, 3)] + [beside(d) for d in range(1, 8)]
    for peer in peers:
        pl.semaphore_signal(barrier, inc=1, device_id=peer, device_id_type=MESH)
    pl.semaphore_wait(barrier, len(peers))

    drains = []
    count = [0]

    def slot():
        count[0] += 1
        assert count[0] <= NSEM
        return count[0] - 1

    def copy_to(src, dst, sem, to, recv=None):
        return pltpu.make_async_remote_copy(
            src_ref=src, dst_ref=dst, send_sem=send_sem.at[0],
            recv_sem=recv_sem.at[sem] if recv is None else recv,
            device_id=to, device_id_type=MESH,
        )

    def send(src, dst, sem, to, recv=None):
        cp = copy_to(src, dst, sem, to, recv)
        cp.start()
        drains.append((None, cp))
        return cp

    def send_if(cond, src, dst, sem, to, recv=None):
        cp = copy_to(src, dst, sem, to, recv)
        pl.when(cond)(cp.start)
        drains.append((cond, cp))
        return cp

    gap_all[g] = gaps[...]
    gap_sems = [slot() for _ in range(3)]
    gap_copies = []
    for d in range(1, 4):
        o = (g + d) % 4
        gap_copies.append(
            send(gaps, gap_all.at[g], gap_sems[d - 1], device(x, z, yh, o // 2, o % 2))
        )

    def turn(i, j):
        start = pl.multiple_of((i * 4 + j) * 128, 128)
        bt[i, j] = basis[:, pl.ds(start, 128)].T

    loads[0].wait()
    loads[1].wait()
    for j in range(4):
        turn((x + 2) % 4, j)

    def block(axis, q, lo, width):
        rows = bt[q] if axis == "x" else bt[:, q]
        return jnp.dot(
            rows.reshape(512, NK), dens[:, lo : lo + width], preferred_element_type=F32
        )

    here = {"x": x, "z": z}
    sem1 = {}

    def first_start(b, axis):
        h = 0 if axis == "x" else 1
        me, lo = here[axis], b * W + h * H
        sems = [slot() for _ in range(3)]
        far, near = s1_far.at[b, h], s1_near.at[b, h]
        if b == 1 and axis == "x":
            loads[5].wait()
        if b == 0 and axis == "z":
            for n, d in enumerate((0, 1, 3)):
                loads[n + 2].wait()
                turn((x + d) % 4, (z + 2) % 4)
        value = block(axis, (me + 2) % 4, lo, H).astype(BF16)
        far[0] = value[:HALF]
        far[1] = value[HALF:]
        recv = s1_recv.at[b, h]
        copies = [
            send(far.at[0], recv.at[0], sems[0], along(axis, 1)),
            send(far.at[1], recv.at[1], sems[1], along(axis, 3)),
        ]
        sem1[b, axis] = (sems, copies)

    def near_part(b, axis):
        h = 0 if axis == "x" else 1
        me, lo = here[axis], b * W + h * H
        sems, copies = sem1[b, axis]
        near, recv = s1_near.at[b, h], s1_recv.at[b, h]
        value = block(axis, (me + 1) % 4, lo, H)
        near[1] = value[HALF:].astype(BF16)
        copies.append(send(near.at[1], recv.at[3], sems[2], along(axis, 1)))
        own_f32[b, h, 0] = value[:HALF]
        value = block(axis, (me + 3) % 4, lo, H)
        near[2] = value[:HALF].astype(BF16)
        copies.append(send(near.at[2], recv.at[4], sems[2], along(axis, 3)))
        own_f32[b, h, 1] = value[HALF:]

    def first_own(b, axis):
        h = 0 if axis == "x" else 1
        me, lo = here[axis], b * W + h * H
        s1_sum[b, h] = block(axis, me, lo, H)

    def first_forward(b, axis):
        h = 0 if axis == "x" else 1
        sems, copies = sem1[b, axis]
        near, recv = s1_near.at[b, h], s1_recv.at[b, h]
        copies[0].wait_recv()
        near[0] = (own_f32[b, h, 0] + recv[0].astype(F32)).astype(BF16)
        copies.append(send(near.at[0], recv.at[2], sems[2], along(axis, 1)))
        copies[1].wait_recv()
        near[3] = (own_f32[b, h, 1] + recv[1].astype(F32)).astype(BF16)
        copies.append(send(near.at[3], recv.at[5], sems[2], along(axis, 3)))

    def first_end(b, axis):
        h = 0 if axis == "x" else 1
        recv = s1_recv.at[b, h]
        last = recv.at[pl.ds(2, 4)]
        copy_to(last, last, sem1[b, axis][0][2], along(axis, 1)).wait_recv()
        total = s1_sum.at[b, h]
        total[:HALF] = total[:HALF] + recv[2].astype(F32) + recv[4].astype(F32)
        total[HALF:] = total[HALF:] + recv[3].astype(F32) + recv[5].astype(F32)

    sem2 = {}

    def second_start(b, axis):
        h = 0 if axis == "x" else 1
        other = "z" if axis == "x" else "x"
        me = here[other]
        sem = slot()
        for i, d in enumerate((2, 1, 3)):
            start = pl.multiple_of((me + d) % 4 * 128, 128)
            s2_send[b, h, i] = s1_sum[b, h, pl.ds(start, 128), :].astype(BF16)
            send(s2_send.at[b, h, i], s2_recv.at[b, h, i], sem, along(other, d))
        sem2[b, axis] = sem

    is_home = g == x
    is_source = is_home
    step = 1 - 2 * (g % 2)
    rel = (x - g + 4) % 4
    is_out1 = rel == (4 - step) % 4
    pair_to = device((g + step + 4) % 4, z, yh, yl, c)
    out1_to = device((g - step + 4) % 4, z, yh, yl, c)
    out2_to = device((g + 2) % 4, z, yh, yl, c)

    def split(b):
        return b in (1, 2)

    sem_y = {}

    def second_end(b, axis):
        h = 0 if axis == "x" else 1
        other = "z" if axis == "x" else "x"
        every = s2_recv.at[b, h]
        copy_to(every, every, sem2[b, axis], along(other, 1)).wait_recv()
        start = pl.multiple_of(here[other] * 128, 128)
        total = s1_sum[b, h, pl.ds(start, 128), :]
        for i in range(3):
            total = total + s2_recv[b, h, i].astype(F32)
        t_own[b, h] = total
        theirs = pl.multiple_of((1 - yh) * 64, 64)
        y_send[b, h] = t_own[b, h, pl.ds(theirs, 64), :].astype(BF16)
        sem_y[b, h] = send(y_send.at[b, h], y_recv.at[b, h], slot(), beside(4))

    own_rows = pl.ds(pl.multiple_of(yh * 64, 64), 64)

    def rows_start(b):
        for h in range(2):
            sem_y[b, h].wait_recv()
            value = (t_own[b, h, own_rows, :] + y_recv[b, h].astype(F32)).astype(BF16)
            proj[:, b * W + h * H : b * W + (h + 1) * H] = value
            ib[b, g, h] = value
        other_home = device(x, z, 1 - yh, x // 2, x % 2)
        for h in range(2):
            cond = yl != yh if h == 1 and split(b) else None
            pair = (ib.at[b, g, h], jb.at[b, z, h, g, own_rows])
            if cond is None:
                send(*pair, 0, other_home, recv=home_sem.at[b, h])
            else:
                send_if(cond, *pair, 0, other_home, recv=home_sem.at[b, h])
        mine = ib.at[b, g]
        send_if(
            g != x, mine, mine, 0, device(x, z, yh, x // 2, x % 2),
            recv=row_sem.at[b],
        )

    def rows_more(b):
        mine = ib.at[b, g]
        for d in range(1, 4):
            o = (g + d) % 4
            send_if(
                o != x, mine, mine, 0, device(x, z, yh, o // 2, o % 2),
                recv=row_sem.at[b],
            )

    def rows_end(b):
        three = ib.at[b, pl.ds(0, 3)]
        copy_to(three, three, 0, along("x", 1), recv=row_sem.at[b]).wait_recv()

    def weigh(b):
        if b == 0:
            for cp in gap_copies:
                cp.wait_recv()
        column = lax.broadcasted_iota(jnp.int32, (NFREQ, W), 0)
        square = jnp.zeros((NFREQ, W), F32)
        for k in range(NFREQ):
            square = jnp.where(column == k, freq[k] * freq[k], square)
        for gg in range(4):
            gap = gap_all[gg, :, b * W : (b + 1) * W]
            value = (-4.0 / PAIRS) * gap / (gap * gap + square)
            for h in range(2):
                wts[b, h, :, gg * H : (gg + 1) * H] = value[:, h * H : (h + 1) * H]

    def scale(b):
        pl.when(jnp.logical_not(is_home))(lambda: rows_end(b))
        for h in range(2):
            rows = jnp.concatenate([ib[b, gg, h] for gg in range(4)], axis=1).astype(F32)

            def at(k, _, h=h, rows=rows):
                start = pl.multiple_of(k * 64, 64)
                scaled[b, h, pl.ds(start, 64), :] = (
                    wts[b, h, pl.ds(k, 1), :] * rows
                ).astype(BF16)
                return 0

            lax.fori_loop(0, NFREQ, at, 0)

    def direct(b):
        return b == NBT - 1

    sem_g = {}
    zn = [z, (z + 3) % 4, (z + 1) % 4, (z + 2) % 4]

    def wait_in(dst, sem, to):
        copy_to(dst, dst, sem, to).wait_recv()

    def part(b, zz, h):
        if h == 1 and split(b):
            return jb.at[b, zz, 1, pl.ds(2 * yh, 2)]
        return jb.at[b, zz, h]

    def half(b, zz, h, n):
        if h == 1 and split(b):
            return jb.at[b, zz, 1, pl.ds(2 * yh + n, 1)]
        return jb.at[b, zz, h, pl.ds(2 * n, 2)]

    def pieces(b, zz, h):
        if h == 1 and split(b):
            return [part(b, zz, h)]
        return [half(b, zz, h, n) for n in range(2)]

    def gather1(b):
        ss = {name + str(h): slot() for name in ("a0", "ab", "b1", "c", "d") for h in range(2)}
        for n in range(2):
            ss["x1", n] = slot()
        for i in range(4):
            for n in range(1 if split(b) else 2):
                ss["x2", i, n] = slot()
            if split(b):
                ss["y2", i] = slot()
        sem_g[b] = ss
        pl.when(is_home)(lambda: rows_end(b))
        for h in range(2):

            @pl.when(is_home)
            def _(h=h):
                groups = [2 * yh, 2 * yh + 1] if h == 1 and split(b) else range(4)
                for gg in groups:
                    jb[b, z, h, gg, own_rows, :] = ib[b, gg, h]
                block = jb.at[b, z, h, pl.ds(0, len(groups)), own_rows]
                copy_to(block, block, 0, along("x", 1), recv=home_sem.at[b, h]).wait_recv()

            if h == 0:
                for n, piece in enumerate(pieces(b, z, 0)):
                    send_if(is_source, piece, piece, ss["x1", n], out1_to)
                    if direct(b):
                        send_if(is_source, piece, piece, ss["x1", n], out2_to)
                    send_if(
                        is_source, piece, piece, ss["x1", n], pair_to
                    )
            else:
                ring_start(b, 1, is_source)

    def ring_start(b, h, cond):
        ss = sem_g[b]
        for n in range(2):
            up, down = half(b, z, h, n), half(b, z, h, 1 - n)
            one = (up, up, ss[("a0", "ab")[n] + str(h)], along("z", 1))
            two = (down, down, ss[("b1", "ab")[n] + str(h)], along("z", 3))
            for args in (one, two):
                if cond is None:
                    send(*args)
                else:
                    send_if(cond, *args)

    def gather2(b):
        ss = sem_g[b]
        for n, piece in enumerate(pieces(b, z, 0)):

            @pl.when(jnp.logical_not(is_source))
            def _(n=n, piece=piece):
                wait_in(piece, ss["x1", n], along("x", 1))

            if not direct(b):
                send_if(is_out1, piece, piece, ss["x1", n], out2_to)
        ring_start(b, 0, None)
        spread2(b, 0)

    def spread2(b, i, which=None):
        ss = sem_g[b]
        for n, piece in enumerate(pieces(b, zn[i], 1)):
            if which is None or n == which:
                send_if(is_source, piece, piece, ss["x2", i, n], out1_to)
                if direct(b):
                    send_if(is_source, piece, piece, ss["x2", i, n], out2_to)
                send_if(
                    is_source, piece, piece, ss["x2", i, n], pair_to
                )

    def pass2(b, i):
        ss = sem_g[b]
        for n, piece in enumerate(pieces(b, zn[i], 1)):

            @pl.when(jnp.logical_not(is_source))
            def _(n=n, piece=piece):
                wait_in(piece, ss["x2", i, n], along("x", 1))

            if not direct(b):
                send_if(is_out1, piece, piece, ss["x2", i, n], out2_to)
        if split(b):
            send(piece, piece, ss["y2", i], beside(4))

    def across_end(b, i):
        wait_in(jb.at[b, zn[i], 1, pl.ds(2 - 2 * yh, 2)], sem_g[b]["y2", i], beside(4))

    def under(cond, go):
        if cond is None:
            go()
        else:
            pl.when(cond)(go)

    def ring_mid(b, h, cond):
        ss = sem_g[b]
        lower, upper = half(b, zn[1], h, 0), half(b, zn[2], h, 1)
        for ref, name, on, d in ((lower, "a0", "c", 1), (upper, "b1", "d", 3)):
            under(cond, lambda ref=ref, name=name: wait_in(ref, ss[f"{name}{h}"], along("z", 1)))
            if cond is None:
                send(ref, ref, ss[f"{on}{h}"], along("z", d))
            else:
                send_if(cond, ref, ref, ss[f"{on}{h}"], along("z", d))
        under(cond, lambda: wait_in(part(b, zn[1], h), ss[f"ab{h}"], along("z", 1)))

    def ring_end(b, h, cond, after=None):
        ss = sem_g[b]
        for n, name in enumerate("cd"):
            ref = half(b, zn[3], h, n)
            under(cond, lambda ref=ref, name=name: wait_in(ref, ss[f"{name}{h}"], along("z", 1)))
            if after is not None:
                after(n)

    def gather3(b):
        ring_mid(b, 1, is_source)
        spread2(b, 1)
        spread2(b, 2)
        pass2(b, 0)
        ring_mid(b, 0, None)

    def gather4(b):
        if split(b):
            ring_end(b, 1, is_source)
            spread2(b, 3)
        else:
            ring_end(b, 1, is_source, lambda n: spread2(b, 3, n))
        pass2(b, 1)
        pass2(b, 2)

    def gather5(b):
        pass2(b, 3)
        ring_end(b, 0, None)

    def multiply(b, h, which, first=False):
        if h == 1 and split(b):
            for i in which:
                across_end(b, i)
        rows = jnp.concatenate(
            [
                jnp.concatenate([jb[b, zn[i], h, gg] for gg in range(4)], axis=1)
                for i in which
            ],
            axis=0,
        )
        value = lax.dot_general(
            scaled[b, h], rows, (((1,), (1,)), ((), ())), preferred_element_type=F32
        )
        for n, i in enumerate(which):
            col = pl.ds(pl.multiple_of(zn[i] * 128, 128), 128)
            share = value[:, n * 128 : (n + 1) * 128]
            if first:
                pol[:, col] = share
            else:
                pol[:, col] += share

    first_start(0, 'x')
    first_start(0, 'z')
    for d in (0, 1, 3):
        for e in (0, 1, 3):
            turn((x + d) % 4, (z + e) % 4)
    near_part(0, 'x')
    near_part(0, 'z')
    first_own(0, 'x')
    first_own(0, 'z')
    first_forward(0, 'x')
    first_forward(0, 'z')
    first_start(1, 'x')
    first_start(1, 'z')
    near_part(1, 'x')
    near_part(1, 'z')
    first_own(1, 'x')
    first_own(1, 'z')
    first_end(0, 'x')
    first_end(0, 'z')
    second_start(0, 'x')
    second_start(0, 'z')
    weigh(0)
    first_forward(1, 'x')
    first_forward(1, 'z')
    first_start(2, 'x')
    first_start(2, 'z')
    near_part(2, 'x')
    near_part(2, 'z')
    first_own(2, 'x')
    first_own(2, 'z')
    second_end(0, 'x')
    second_end(0, 'z')
    first_end(1, 'x')
    first_end(1, 'z')
    second_start(1, 'x')
    second_start(1, 'z')
    weigh(1)
    first_forward(2, 'x')
    first_forward(2, 'z')
    first_start(3, 'x')
    first_start(3, 'z')
    near_part(3, 'x')
    near_part(3, 'z')
    first_own(3, 'x')
    first_own(3, 'z')
    rows_start(0)
    second_end(1, 'x')
    second_end(1, 'z')
    first_end(2, 'x')
    first_end(2, 'z')
    second_start(2, 'x')
    second_start(2, 'z')
    weigh(2)
    first_forward(3, 'x')
    first_forward(3, 'z')
    gather1(0)
    rows_start(1)
    second_end(2, 'x')
    second_end(2, 'z')
    first_end(3, 'x')
    first_end(3, 'z')
    second_start(3, 'x')
    second_start(3, 'z')
    weigh(3)
    gather2(0)
    rows_more(0)
    rows_start(2)
    gather1(1)
    second_end(3, 'x')
    second_end(3, 'z')
    gather3(0)
    scale(0)
    gather2(1)
    rows_more(1)
    rows_start(3)
    gather4(0)
    gather1(2)
    multiply(0, 0, (0, 1), first=True)
    gather3(1)
    gather5(0)
    scale(1)
    gather2(2)
    multiply(0, 0, (2, 3), first=True)
    multiply(0, 1, (0, 1))
    rows_more(2)
    gather4(1)
    gather1(3)
    multiply(1, 0, (0, 1))
    gather3(2)
    multiply(0, 1, (2, 3))
    gather5(1)
    scale(2)
    gather2(3)
    multiply(1, 0, (2, 3))
    multiply(1, 1, (0, 1))
    rows_more(3)
    gather4(2)
    multiply(2, 0, (0, 1))
    gather3(3)
    multiply(1, 1, (2, 3))
    gather5(2)
    scale(3)
    multiply(2, 0, (2, 3))
    multiply(2, 1, (0, 1))
    gather4(3)
    multiply(3, 0, (0, 1))
    multiply(2, 1, (2, 3))
    gather5(3)
    multiply(3, 0, (2, 3))
    multiply(3, 1, (0, 1))
    multiply(3, 1, (2, 3))
    for cond, cp in drains:
        if cond is None:
            cp.wait_send()
        else:
            pl.when(cond)(cp.wait_send)


def on_device(basis_set, densities, pair_gaps, frequencies):
    any_, vmem = pl.BlockSpec(memory_space=pl.ANY), pl.BlockSpec(memory_space=pltpu.VMEM)
    pol, proj = pl.pallas_call(
        kernel,
        out_shape=(
            pltpu.VMEM((NFREQ * 64, 512), F32),
            pltpu.VMEM((64, NP), BF16),
        ),
        in_specs=[any_, any_, vmem, pl.BlockSpec(memory_space=pltpu.SMEM)],
        out_specs=(vmem, vmem),
        scratch_shapes=[
            pltpu.VMEM((NK, NB), BF16),
            pltpu.VMEM((NK, NP), BF16),
            pltpu.VMEM((4, 4, 128, NK), BF16),
            pltpu.VMEM((NBT, 2, 2, HALF, H), F32),
            pltpu.VMEM((NBT, 2, 6, HALF, H), BF16),
            pltpu.VMEM((NBT, 2, 2, HALF, H), BF16),
            pltpu.VMEM((NBT, 2, 4, HALF, H), BF16),
            pltpu.VMEM((NBT, 2, 512, H), F32),
            pltpu.VMEM((NBT, 2, 3, 128, H), BF16),
            pltpu.VMEM((NBT, 2, 3, 128, H), BF16),
            pltpu.VMEM((NBT, 2, 128, H), F32),
            pltpu.VMEM((NBT, 2, 64, H), BF16),
            pltpu.VMEM((NBT, 2, 64, H), BF16),
            pltpu.VMEM((NBT, 4, 2, 64, H), BF16),
            pltpu.VMEM((4, 1, NP), F32),
            pltpu.VMEM((NBT, 2, NFREQ, 2 * W), F32),
            pltpu.VMEM((NBT, 2, NFREQ * 64, 2 * W), BF16),
            pltpu.VMEM((NBT, 4, 2, 4, 128, H), BF16),
            pltpu.SemaphoreType.DMA((6,)),
            pltpu.SemaphoreType.DMA((1,)),
            pltpu.SemaphoreType.DMA((NSEM,)),
            pltpu.SemaphoreType.DMA((NBT, 2)),
            pltpu.SemaphoreType.DMA((NBT,)),
        ],
        compiler_params=pltpu.CompilerParams(
            collective_id=0, has_side_effects=True, vmem_limit_bytes=56 * 2**20
        ),
    )(basis_set, densities, pair_gaps.reshape(1, NP), frequencies)
    return pol.reshape(NFREQ, 64, 512), proj


def solution(mesh):
    in_specs = (P("pw", None), P("pw", "band"), P("band"), P())
    out_specs = (P(None, "pw", "band"), P("pw", "band"))
    return jax.shard_map(
        on_device, mesh=mesh, in_specs=in_specs, out_specs=out_specs, check_vma=False
    )
```

```python
import functools

import jax
import jax.numpy as jnp
from jax import lax
from jax.experimental import pallas as pl
from jax.experimental.pallas import tpu as pltpu
from jax.sharding import PartitionSpec as P

MESH = pl.DeviceIdType.MESH
F32, BF16 = jnp.float32, jnp.bfloat16

NK = 768
NB = 2048
NP = 1024
NFREQ = 16
PAIRS = 4096
NBT = 4
W = NP // NBT
H = W // 2
HALF = 256
NSEM = 3 + NBT * 32


def device(x, z, yh, yl, c):
    return ((x * 4 + z) * 2 + yh, yl * 2 + c)


def kernel(
    basis_hbm, dens_hbm, gaps, freq,
    pol, proj,
    basis, dens, bt,
    own_f32, s1_recv, s1_far, s1_near, s1_sum,
    s2_send, s2_recv,
    t_own, y_send, y_recv,
    ib, gap_all, wts, scaled, jb,
    load_sem, send_sem, recv_sem, home_sem, row_sem,
):
    pw, g = lax.axis_index("pw"), lax.axis_index("band")
    x, z, yh = pw // 8, (pw // 2) % 4, pw % 2
    yl, c = g // 2, g % 2
    me8 = yh * 4 + g

    def fetch(src, dst, cols, n):
        return pltpu.make_async_copy(src.at[:, cols], dst.at[:, cols], load_sem.at[n])

    loads = [fetch(dens_hbm, dens, pl.ds(0, W), 0)]
    for n, d in enumerate((2, 0, 1, 3)):
        cols = pl.ds(pl.multiple_of((x + d) % 4 * 512, 512), 512)
        loads.append(fetch(basis_hbm, basis, cols, n + 1))
    loads.append(fetch(dens_hbm, dens, pl.ds(W, NP - W), 5))
    for load in loads:
        load.start()

    def along(axis, d):
        if axis == "x":
            return device((x + d) % 4, z, yh, yl, c)
        return device(x, (z + d) % 4, yh, yl, c)

    def beside(d):
        o = (me8 + d) % 8
        return device(x, z, o // 4, (o % 4) // 2, o % 2)

    barrier = pltpu.get_barrier_semaphore()
    peers = [along(a, d) for a in "xz" for d in (1, 2, 3)] + [beside(d) for d in range(1, 8)]
    for peer in peers:
        pl.semaphore_signal(barrier, inc=1, device_id=peer, device_id_type=MESH)
    pl.semaphore_wait(barrier, len(peers))

    drains = []
    count = [0]

    def slot():
        count[0] += 1
        assert count[0] <= NSEM
        return count[0] - 1

    def copy_to(src, dst, sem, to, recv=None):
        return pltpu.make_async_remote_copy(
            src_ref=src, dst_ref=dst, send_sem=send_sem.at[0],
            recv_sem=recv_sem.at[sem] if recv is None else recv,
            device_id=to, device_id_type=MESH,
        )

    def send(src, dst, sem, to, recv=None):
        cp = copy_to(src, dst, sem, to, recv)
        cp.start()
        drains.append((None, cp))
        return cp

    def send_if(cond, src, dst, sem, to, recv=None):
        cp = copy_to(src, dst, sem, to, recv)
        pl.when(cond)(cp.start)
        drains.append((cond, cp))
        return cp

    gap_all[g] = gaps[...]
    gap_sems = [slot() for _ in range(3)]
    gap_copies = []
    for d in range(1, 4):
        o = (g + d) % 4
        gap_copies.append(
            send(gaps, gap_all.at[g], gap_sems[d - 1], device(x, z, yh, o // 2, o % 2))
        )

    def turn(i, j):
        start = pl.multiple_of((i * 4 + j) * 128, 128)
        bt[i, j] = basis[:, pl.ds(start, 128)].T

    loads[0].wait()
    loads[1].wait()
    for j in range(4):
        turn((x + 2) % 4, j)

    def block(axis, q, lo, width):
        rows = bt[q] if axis == "x" else bt[:, q]
        return jnp.dot(
            rows.reshape(512, NK), dens[:, lo : lo + width], preferred_element_type=F32
        )

    here = {"x": x, "z": z}
    sem1 = {}

    def first_start(b, axis):
        h = 0 if axis == "x" else 1
        me, lo = here[axis], b * W + h * H
        sems = [slot() for _ in range(3)]
        far, near = s1_far.at[b, h], s1_near.at[b, h]
        if b == 1 and axis == "x":
            loads[5].wait()
        if b == 0 and axis == "z":
            for n, d in enumerate((0, 1, 3)):
                loads[n + 2].wait()
                turn((x + d) % 4, (z + 2) % 4)
        value = block(axis, (me + 2) % 4, lo, H).astype(BF16)
        far[0] = value[:HALF]
        far[1] = value[HALF:]
        recv = s1_recv.at[b, h]
        copies = [
            send(far.at[0], recv.at[0], sems[0], along(axis, 1)),
            send(far.at[1], recv.at[1], sems[1], along(axis, 3)),
        ]
        sem1[b, axis] = (sems, copies)

    def near_part(b, axis):
        h = 0 if axis == "x" else 1
        me, lo = here[axis], b * W + h * H
        sems, copies = sem1[b, axis]
        near, recv = s1_near.at[b, h], s1_recv.at[b, h]
        value = block(axis, (me + 1) % 4, lo, H)
        near[1] = value[HALF:].astype(BF16)
        copies.append(send(near.at[1], recv.at[3], sems[2], along(axis, 1)))
        own_f32[b, h, 0] = value[:HALF]
        value = block(axis, (me + 3) % 4, lo, H)
        near[2] = value[:HALF].astype(BF16)
        copies.append(send(near.at[2], recv.at[4], sems[2], along(axis, 3)))
        own_f32[b, h, 1] = value[HALF:]

    def first_own(b, axis):
        h = 0 if axis == "x" else 1
        me, lo = here[axis], b * W + h * H
        s1_sum[b, h] = block(axis, me, lo, H)

    def first_forward(b, axis):
        h = 0 if axis == "x" else 1
        sems, copies = sem1[b, axis]
        near, recv = s1_near.at[b, h], s1_recv.at[b, h]
        copies[0].wait_recv()
        near[0] = (own_f32[b, h, 0] + recv[0].astype(F32)).astype(BF16)
        copies.append(send(near.at[0], recv.at[2], sems[2], along(axis, 1)))
        copies[1].wait_recv()
        near[3] = (own_f32[b, h, 1] + recv[1].astype(F32)).astype(BF16)
        copies.append(send(near.at[3], recv.at[5], sems[2], along(axis, 3)))

    def first_end(b, axis):
        h = 0 if axis == "x" else 1
        recv = s1_recv.at[b, h]
        last = recv.at[pl.ds(2, 4)]
        copy_to(last, last, sem1[b, axis][0][2], along(axis, 1)).wait_recv()
        total = s1_sum.at[b, h]
        total[:HALF] = total[:HALF] + recv[2].astype(F32) + recv[4].astype(F32)
        total[HALF:] = total[HALF:] + recv[3].astype(F32) + recv[5].astype(F32)

    sem2 = {}

    def second_start(b, axis):
        h = 0 if axis == "x" else 1
        other = "z" if axis == "x" else "x"
        me = here[other]
        sem = slot()
        for i, d in enumerate((2, 1, 3)):
            start = pl.multiple_of((me + d) % 4 * 128, 128)
            s2_send[b, h, i] = s1_sum[b, h, pl.ds(start, 128), :].astype(BF16)
            send(s2_send.at[b, h, i], s2_recv.at[b, h, i], sem, along(other, d))
        sem2[b, axis] = sem

    is_home = g == x
    is_source = is_home
    step = 1 - 2 * (g % 2)
    rel = (x - g + 4) % 4
    is_out1 = rel == (4 - step) % 4
    pair_to = device((g + step + 4) % 4, z, yh, yl, c)
    out1_to = device((g - step + 4) % 4, z, yh, yl, c)
    out2_to = device((g + 2) % 4, z, yh, yl, c)

    def split(b):
        return b in (1, 2)

    sem_y = {}

    def second_end(b, axis):
        h = 0 if axis == "x" else 1
        other = "z" if axis == "x" else "x"
        every = s2_recv.at[b, h]
        copy_to(every, every, sem2[b, axis], along(other, 1)).wait_recv()
        start = pl.multiple_of(here[other] * 128, 128)
        total = s1_sum[b, h, pl.ds(start, 128), :]
        for i in range(3):
            total = total + s2_recv[b, h, i].astype(F32)
        t_own[b, h] = total
        theirs = pl.multiple_of((1 - yh) * 64, 64)
        y_send[b, h] = t_own[b, h, pl.ds(theirs, 64), :].astype(BF16)
        sem_y[b, h] = send(y_send.at[b, h], y_recv.at[b, h], slot(), beside(4))

    own_rows = pl.ds(pl.multiple_of(yh * 64, 64), 64)

    def rows_start(b):
        for h in range(2):
            sem_y[b, h].wait_recv()
            value = (t_own[b, h, own_rows, :] + y_recv[b, h].astype(F32)).astype(BF16)
            proj[:, b * W + h * H : b * W + (h + 1) * H] = value
            ib[b, g, h] = value
        other_home = device(x, z, 1 - yh, x // 2, x % 2)
        for h in range(2):
            cond = yl != yh if h == 1 and split(b) else None
            pair = (ib.at[b, g, h], jb.at[b, z, h, g, own_rows])
            if cond is None:
                send(*pair, 0, other_home, recv=home_sem.at[b, h])
            else:
                send_if(cond, *pair, 0, other_home, recv=home_sem.at[b, h])
        mine = ib.at[b, g]
        send_if(
            g != x, mine, mine, 0, device(x, z, yh, x // 2, x % 2),
            recv=row_sem.at[b],
        )

    def rows_more(b):
        mine = ib.at[b, g]
        for d in range(1, 4):
            o = (g + d) % 4
            send_if(
                o != x, mine, mine, 0, device(x, z, yh, o // 2, o % 2),
                recv=row_sem.at[b],
            )

    def rows_end(b):
        three = ib.at[b, pl.ds(0, 3)]
        copy_to(three, three, 0, along("x", 1), recv=row_sem.at[b]).wait_recv()

    def weigh(b):
        if b == 0:
            for cp in gap_copies:
                cp.wait_recv()
        column = lax.broadcasted_iota(jnp.int32, (NFREQ, W), 0)
        square = jnp.zeros((NFREQ, W), F32)
        for k in range(NFREQ):
            square = jnp.where(column == k, freq[k] * freq[k], square)
        for gg in range(4):
            gap = gap_all[gg, :, b * W : (b + 1) * W]
            value = (-4.0 / PAIRS) * gap / (gap * gap + square)
            for h in range(2):
                wts[b, h, :, gg * H : (gg + 1) * H] = value[:, h * H : (h + 1) * H]

    def scale(b):
        pl.when(jnp.logical_not(is_home))(lambda: rows_end(b))
        for h in range(2):
            rows = jnp.concatenate([ib[b, gg, h] for gg in range(4)], axis=1).astype(F32)

            def at(k, _, h=h, rows=rows):
                start = pl.multiple_of(k * 64, 64)
                scaled[b, h, pl.ds(start, 64), :] = (
                    wts[b, h, pl.ds(k, 1), :] * rows
                ).astype(BF16)
                return 0

            lax.fori_loop(0, NFREQ, at, 0)

    def direct(b):
        return b == NBT - 1

    sem_g = {}
    zn = [z, (z + 3) % 4, (z + 1) % 4, (z + 2) % 4]

    def wait_in(dst, sem, to):
        copy_to(dst, dst, sem, to).wait_recv()

    def part(b, zz, h):
        if h == 1 and split(b):
            return jb.at[b, zz, 1, pl.ds(2 * yh, 2)]
        return jb.at[b, zz, h]

    def half(b, zz, h, n):
        if h == 1 and split(b):
            return jb.at[b, zz, 1, pl.ds(2 * yh + n, 1)]
        return jb.at[b, zz, h, pl.ds(2 * n, 2)]

    def pieces(b, zz, h):
        if h == 1 and split(b):
            return [part(b, zz, h)]
        return [half(b, zz, h, n) for n in range(2)]

    def gather1(b):
        ss = {name + str(h): slot() for name in ("a0", "ab", "b1", "c", "d") for h in range(2)}
        for n in range(2):
            ss["x1", n] = slot()
        for i in range(4):
            for n in range(1 if split(b) else 2):
                ss["x2", i, n] = slot()
            if split(b):
                ss["y2", i] = slot()
        sem_g[b] = ss
        pl.when(is_home)(lambda: rows_end(b))
        for h in range(2):

            @pl.when(is_home)
            def _(h=h):
                groups = [2 * yh, 2 * yh + 1] if h == 1 and split(b) else range(4)
                for gg in groups:
                    jb[b, z, h, gg, own_rows, :] = ib[b, gg, h]
                block = jb.at[b, z, h, pl.ds(0, len(groups)), own_rows]
                copy_to(block, block, 0, along("x", 1), recv=home_sem.at[b, h]).wait_recv()

            if h == 0:
                for n, piece in enumerate(pieces(b, z, 0)):
                    send_if(is_source, piece, piece, ss["x1", n], out1_to)
                    if direct(b):
                        send_if(is_source, piece, piece, ss["x1", n], out2_to)
                    send_if(
                        is_source, piece, piece, ss["x1", n], pair_to
                    )
            else:
                ring_start(b, 1, is_source)

    def ring_start(b, h, cond):
        ss = sem_g[b]
        for n in range(2):
            up, down = half(b, z, h, n), half(b, z, h, 1 - n)
            one = (up, up, ss[("a0", "ab")[n] + str(h)], along("z", 1))
            two = (down, down, ss[("b1", "ab")[n] + str(h)], along("z", 3))
            for args in (one, two):
                if cond is None:
                    send(*args)
                else:
                    send_if(cond, *args)

    def gather2(b):
        ss = sem_g[b]
        for n, piece in enumerate(pieces(b, z, 0)):

            @pl.when(jnp.logical_not(is_source))
            def _(n=n, piece=piece):
                wait_in(piece, ss["x1", n], along("x", 1))

            if not direct(b):
                send_if(is_out1, piece, piece, ss["x1", n], out2_to)
        ring_start(b, 0, None)
        spread2(b, 0)

    def spread2(b, i, which=None):
        ss = sem_g[b]
        for n, piece in enumerate(pieces(b, zn[i], 1)):
            if which is None or n == which:
                send_if(is_source, piece, piece, ss["x2", i, n], out1_to)
                if direct(b):
                    send_if(is_source, piece, piece, ss["x2", i, n], out2_to)
                send_if(
                    is_source, piece, piece, ss["x2", i, n], pair_to
                )

    def pass2(b, i):
        ss = sem_g[b]
        for n, piece in enumerate(pieces(b, zn[i], 1)):

            @pl.when(jnp.logical_not(is_source))
            def _(n=n, piece=piece):
                wait_in(piece, ss["x2", i, n], along("x", 1))

            if not direct(b):
                send_if(is_out1, piece, piece, ss["x2", i, n], out2_to)
        if split(b):
            send(piece, piece, ss["y2", i], beside(4))

    def across_end(b, i):
        wait_in(jb.at[b, zn[i], 1, pl.ds(2 - 2 * yh, 2)], sem_g[b]["y2", i], beside(4))

    def under(cond, go):
        if cond is None:
            go()
        else:
            pl.when(cond)(go)

    def ring_mid(b, h, cond):
        ss = sem_g[b]
        lower, upper = half(b, zn[1], h, 0), half(b, zn[2], h, 1)
        for ref, name, on, d in ((lower, "a0", "c", 1), (upper, "b1", "d", 3)):
            under(cond, lambda ref=ref, name=name: wait_in(ref, ss[f"{name}{h}"], along("z", 1)))
            if cond is None:
                send(ref, ref, ss[f"{on}{h}"], along("z", d))
            else:
                send_if(cond, ref, ref, ss[f"{on}{h}"], along("z", d))
        under(cond, lambda: wait_in(part(b, zn[1], h), ss[f"ab{h}"], along("z", 1)))

    def ring_end(b, h, cond, after=None):
        ss = sem_g[b]
        for n, name in enumerate("cd"):
            ref = half(b, zn[3], h, n)
            under(cond, lambda ref=ref, name=name: wait_in(ref, ss[f"{name}{h}"], along("z", 1)))
            if after is not None:
                after(n)

    def gather3(b):
        ring_mid(b, 1, is_source)
        spread2(b, 1)
        spread2(b, 2)
        pass2(b, 0)
        ring_mid(b, 0, None)

    def gather4(b):
        if split(b):
            ring_end(b, 1, is_source)
            spread2(b, 3)
        else:
            ring_end(b, 1, is_source, lambda n: spread2(b, 3, n))
        pass2(b, 1)
        pass2(b, 2)

    def gather5(b):
        pass2(b, 3)
        ring_end(b, 0, None)

    def multiply(b, h, which, first=False):
        if h == 1 and split(b):
            for i in which:
                across_end(b, i)
        rows = jnp.concatenate(
            [
                jnp.concatenate([jb[b, zn[i], h, gg] for gg in range(4)], axis=1)
                for i in which
            ],
            axis=0,
        )
        value = lax.dot_general(
            scaled[b, h], rows, (((1,), (1,)), ((), ())), preferred_element_type=F32
        )
        for n, i in enumerate(which):
            col = pl.ds(pl.multiple_of(zn[i] * 128, 128), 128)
            share = value[:, n * 128 : (n + 1) * 128]
            if first:
                pol[:, col] = share
            else:
                pol[:, col] += share

    first_start(0, 'x')
    first_start(0, 'z')
    for d in (0, 1, 3):
        for e in (0, 1, 3):
            turn((x + d) % 4, (z + e) % 4)
    near_part(0, 'x')
    near_part(0, 'z')
    first_own(0, 'x')
    first_own(0, 'z')
    first_forward(0, 'x')
    first_forward(0, 'z')
    first_start(1, 'x')
    first_start(1, 'z')
    near_part(1, 'x')
    near_part(1, 'z')
    first_own(1, 'x')
    first_own(1, 'z')
    first_end(0, 'x')
    first_end(0, 'z')
    second_start(0, 'x')
    second_start(0, 'z')
    weigh(0)
    first_forward(1, 'x')
    first_forward(1, 'z')
    first_start(2, 'x')
    first_start(2, 'z')
    near_part(2, 'x')
    near_part(2, 'z')
    first_own(2, 'x')
    first_own(2, 'z')
    second_end(0, 'x')
    second_end(0, 'z')
    first_end(1, 'x')
    first_end(1, 'z')
    second_start(1, 'x')
    second_start(1, 'z')
    weigh(1)
    first_forward(2, 'x')
    first_forward(2, 'z')
    first_start(3, 'x')
    first_start(3, 'z')
    near_part(3, 'x')
    near_part(3, 'z')
    first_own(3, 'x')
    first_own(3, 'z')
    rows_start(0)
    second_end(1, 'x')
    second_end(1, 'z')
    first_end(2, 'x')
    first_end(2, 'z')
    second_start(2, 'x')
    second_start(2, 'z')
    weigh(2)
    first_forward(3, 'x')
    first_forward(3, 'z')
    gather1(0)
    rows_start(1)
    second_end(2, 'x')
    second_end(2, 'z')
    first_end(3, 'x')
    first_end(3, 'z')
    second_start(3, 'x')
    second_start(3, 'z')
    weigh(3)
    gather2(0)
    rows_more(0)
    rows_start(2)
    gather1(1)
    second_end(3, 'x')
    second_end(3, 'z')
    gather3(0)
    scale(0)
    gather2(1)
    rows_more(1)
    rows_start(3)
    gather4(0)
    gather1(2)
    multiply(0, 0, (0, 1), first=True)
    gather3(1)
    gather5(0)
    scale(1)
    gather2(2)
    multiply(0, 0, (2, 3), first=True)
    multiply(0, 1, (0, 1))
    rows_more(2)
    gather4(1)
    gather1(3)
    multiply(1, 0, (0, 1))
    gather3(2)
    multiply(0, 1, (2, 3))
    gather5(1)
    scale(2)
    gather2(3)
    multiply(1, 0, (2, 3))
    multiply(1, 1, (0, 1))
    rows_more(3)
    gather4(2)
    multiply(2, 0, (0, 1))
    gather3(3)
    multiply(1, 1, (2, 3))
    gather5(2)
    scale(3)
    multiply(2, 0, (2, 3))
    multiply(2, 1, (0, 1))
    gather4(3)
    multiply(3, 0, (0, 1))
    multiply(2, 1, (2, 3))
    multiply(3, 1, (0, 1))
    ring_end(3, 0, None)
    multiply(3, 0, (2, 3))
    pass2(3, 3)
    multiply(3, 1, (2, 3))
    for cond, cp in drains:
        if cond is None:
            cp.wait_send()
        else:
            pl.when(cond)(cp.wait_send)


def on_device(basis_set, densities, pair_gaps, frequencies):
    any_, vmem = pl.BlockSpec(memory_space=pl.ANY), pl.BlockSpec(memory_space=pltpu.VMEM)
    pol, proj = pl.pallas_call(
        kernel,
        out_shape=(
            pltpu.VMEM((NFREQ * 64, 512), F32),
            pltpu.VMEM((64, NP), BF16),
        ),
        in_specs=[any_, any_, vmem, pl.BlockSpec(memory_space=pltpu.SMEM)],
        out_specs=(vmem, vmem),
        scratch_shapes=[
            pltpu.VMEM((NK, NB), BF16),
            pltpu.VMEM((NK, NP), BF16),
            pltpu.VMEM((4, 4, 128, NK), BF16),
            pltpu.VMEM((NBT, 2, 2, HALF, H), F32),
            pltpu.VMEM((NBT, 2, 6, HALF, H), BF16),
            pltpu.VMEM((NBT, 2, 2, HALF, H), BF16),
            pltpu.VMEM((NBT, 2, 4, HALF, H), BF16),
            pltpu.VMEM((NBT, 2, 512, H), F32),
            pltpu.VMEM((NBT, 2, 3, 128, H), BF16),
            pltpu.VMEM((NBT, 2, 3, 128, H), BF16),
            pltpu.VMEM((NBT, 2, 128, H), F32),
            pltpu.VMEM((NBT, 2, 64, H), BF16),
            pltpu.VMEM((NBT, 2, 64, H), BF16),
            pltpu.VMEM((NBT, 4, 2, 64, H), BF16),
            pltpu.VMEM((4, 1, NP), F32),
            pltpu.VMEM((NBT, 2, NFREQ, 2 * W), F32),
            pltpu.VMEM((NBT, 2, NFREQ * 64, 2 * W), BF16),
            pltpu.VMEM((NBT, 4, 2, 4, 128, H), BF16),
            pltpu.SemaphoreType.DMA((6,)),
            pltpu.SemaphoreType.DMA((1,)),
            pltpu.SemaphoreType.DMA((NSEM,)),
            pltpu.SemaphoreType.DMA((NBT, 2)),
            pltpu.SemaphoreType.DMA((NBT,)),
        ],
        compiler_params=pltpu.CompilerParams(
            collective_id=0, has_side_effects=True, vmem_limit_bytes=56 * 2**20
        ),
    )(basis_set, densities, pair_gaps.reshape(1, NP), frequencies)
    return pol.reshape(NFREQ, 64, 512), proj


def solution(mesh):
    in_specs = (P("pw", None), P("pw", "band"), P("band"), P())
    out_specs = (P(None, "pw", "band"), P("pw", "band"))
    return jax.shard_map(
        on_device, mesh=mesh, in_specs=in_specs, out_specs=out_specs, check_vma=False
    )
```
